256 devices in a mesh: rows: 4 (over x), cols: 64 (over z, y, core).
Axes of the slice: x: 4, y: 4, z: 8, core: 2. Of those that a mesh axis runs over, the one named last changes fastest.
Arguments:
- images: bfloat16 [2, 64, 256, 8192], P(None, None, 'rows', 'cols'), may hold values from -6 to 6
- first_weight: bfloat16 [9, 64, 64], replicated, may hold values from -0.25 to 0.25
- second_weight: bfloat16 [9, 64, 64], replicated, may hold values from -0.25 to 0.25
- search_ranges: int32 [2, 32, 64], P(None, 'rows', 'cols'), may hold values from 0 to 16, as said below
Outputs:
- matched: bfloat16 [64, 256, 8192], P(None, 'rows', 'cols')
- disparity: float32 [256, 8192], P('rows', 'cols')
The draws below stay inside these ranges and needn't reach their ends.
Inputs may be any that keep to these rules, and one draw needn't show every extreme that they name: search_ranges[0] is 0 to 1 and search_ranges[1] is 1 to 16; some block has search_ranges[0] = 1 together with search_ranges[1] = 16.
All inputs are finite; a program needn't handle non-finite values.
Results may differ from the reference program's by a relative error of at most 0.008.
Values may be sent and summed in bfloat16 or wider, within the bound.
A program may use at most 128 MiB of HBM per device.

```python
import jax
import jax.numpy as jnp
from jax import lax

C = 64
SEG = 128
RG = 8
MINB = 2
CNTB = 16
FIRST_DILATION = 2
SECOND_DILATION = 4
HOPS = 18
H = 256
W = 8192
GROUPS = 32
BLOCKS = 64


def draw_search_ranges(key, part):
    folded = jax.random.fold_in(key, 7)
    first_key, second_key, third_key = jax.random.split(folded, 3)
    lowest_blocks = jax.random.randint(first_key, (GROUPS * BLOCKS,), 0, MINB)
    powers = jax.random.randint(second_key, (GROUPS * BLOCKS,), 0, 5)
    counts = jnp.minimum(jnp.left_shift(jnp.ones_like(powers), powers), CNTB)
    chosen = jax.random.randint(third_key, (), 0, GROUPS * BLOCKS)
    spot_mask = jnp.arange(GROUPS * BLOCKS) == chosen
    lowest_blocks = jnp.where(spot_mask, MINB - 1, lowest_blocks)
    counts = jnp.where(spot_mask, CNTB, counts)
    return jnp.stack([lowest_blocks, counts]).reshape(2, GROUPS, BLOCKS).astype(jnp.int32)


def block_scale(key, dims, pieces, least, top_value):
    def one(position, blocks):
        heights = jax.random.uniform(jax.random.fold_in(jax.random.fold_in(key, 6), position), (blocks,), jnp.float32, least / len(pieces), top_value / len(pieces))
        return jnp.repeat(jnp.exp(heights), dims[position] // blocks).reshape((-1,) + (1,) * (len(dims) - position - 1))

    gain = one(*pieces[0])
    for cut in pieces[1:]:
        gain = gain * one(*cut)
    return gain


def normal_values(own_key, extent, scale, bound, pieces=(), kind=jnp.bfloat16):
    array = scale * jax.random.normal(own_key, extent, jnp.float32)
    if pieces:
        array = array * block_scale(own_key, extent, pieces, -0.22, 0.18)
    return jnp.clip(array, -bound, bound).astype(kind)


def setup_inputs(seed: int = 0) -> dict:
    keys = jax.random.split(jax.random.key(seed), 5)
    return {
        "images": normal_values(keys[0], (2, C, H, W), 1.0, 6.0, ((2, 4), (3, 64))),
        "first_weight": normal_values(keys[1], (9, C, C), (9 * C) ** -0.5, 0.25),
        "second_weight": normal_values(keys[2], (9, C, C), (9 * C) ** -0.5, 0.25),
        "search_ranges": draw_search_ranges(jax.random.fold_in(keys[4], 71), 0),
    }


sharpness_divisor = 10.0
epsilon = 1e-05

def apply_convolution(images, weights, dilation):
    height = images.shape[2]
    full_width = images.shape[3]
    padded = jnp.pad(images.astype(jnp.float32), ((0, 0), (0, 0), (dilation, dilation), (dilation, dilation)))
    summed = jnp.zeros((images.shape[0], weights.shape[1], height, full_width), jnp.float32)
    for row_tap in range(3):
        for horizontal_offset in range(3):
            window = padded[:, :, row_tap * dilation:row_tap * dilation + height, horizontal_offset * dilation:horizontal_offset * dilation + full_width]
            summed = summed + jnp.einsum('oc,nchw->nohw', weights[3 * row_tap + horizontal_offset].astype(jnp.float32), window)
    return summed

def normalize(feature_maps):
    widened = feature_maps.astype(jnp.float32)
    return (widened * lax.rsqrt(lax.optimization_barrier(jnp.mean(widened * widened, axis=1, keepdims=True)) + epsilon)).astype(jnp.bfloat16)

def reference(images, first_weight, second_weight, search_ranges):
    inner_activations = jax.nn.silu(apply_convolution(images, first_weight, FIRST_DILATION)).astype(jnp.bfloat16)
    feature_maps = (images.astype(jnp.float32) + apply_convolution(inner_activations, second_weight, SECOND_DILATION)).astype(jnp.bfloat16)
    unit_feats = normalize(feature_maps)
    left_unit = unit_feats[0]
    right_unit = unit_feats[1]
    plane_total, height, full_width = left_unit.shape
    padded = jnp.pad(right_unit, ((0, 0), (0, 0), ((HOPS - 1) * SEG, 0)))
    per_row = jnp.repeat(search_ranges, RG, axis=1)
    offsets = (HOPS - 1) * SEG + jnp.arange(SEG, dtype=jnp.int32)[:, None] - jnp.arange(HOPS * SEG, dtype=jnp.int32)[None, :]

    def one_block(block_index):
        start = (block_index * SEG).astype(jnp.int32)
        source_descriptors = lax.dynamic_slice_in_dim(left_unit, start, SEG, 2).astype(jnp.float32)
        target_descriptors = lax.dynamic_slice_in_dim(padded, start, HOPS * SEG, 2).astype(jnp.float32)
        pairing_similarity = jnp.einsum('yrm,yrs->rms', source_descriptors, target_descriptors) * (sharpness_divisor / plane_total)
        interval_bounds = lax.dynamic_slice_in_dim(per_row, block_index.astype(jnp.int32), 1, 2)[:, :, 0]
        low_edge = SEG * interval_bounds[0]
        high_edge = SEG * (interval_bounds[0] + interval_bounds[1])
        inside = (offsets[None] >= low_edge[:, None, None]) & (offsets[None] < high_edge[:, None, None])
        rounded = lax.optimization_barrier(jnp.where(inside, jnp.exp(pairing_similarity), 0.0).astype(jnp.bfloat16))
        weights = rounded.astype(jnp.float32)
        norm_sum = lax.optimization_barrier(jnp.sum(weights, axis=-1))
        shift_sum = lax.optimization_barrier(jnp.sum(weights * offsets.astype(jnp.float32)[None], axis=-1))
        feature_sum = jnp.einsum('him,chm->chi', weights, target_descriptors)
        return ((feature_sum / norm_sum[None]).astype(jnp.bfloat16), shift_sum / norm_sum / SEG)
    matched, disparity = lax.map(one_block, jnp.arange(full_width // SEG, dtype=jnp.int32))
    matched = matched.transpose(1, 2, 0, 3).reshape(plane_total, height, full_width)
    disparity = disparity.transpose(1, 0, 2).reshape(height, full_width)
    return (matched, disparity)
```

```python
import functools

import jax
import jax.numpy as jnp
from jax import lax
from jax.experimental import pallas as pl
from jax.experimental.pallas import tpu as pltpu
from jax.sharding import PartitionSpec as P

C = 64
SEG = 128
RG = 8
D1 = 2
D2 = 4
EPS = 1e-05
SHARP = 10.0
LOG2E = 1.4426950408889634
ROWS = 64
HALO = D1 + D2
SLOTS = 8
SLOT_ROWS = (ROWS + 2 * D2) // SLOTS
EDGE_TILES = SLOT_ROWS + 2 * D1
IMG_ROWS = ROWS + 2 * HALO
HID_ROWS = ROWS + 2 * D2
PLANE = 8
KEYS = 2 * PLANE + 1
VROWS = 80


def lane_iota(shape):
    return lax.broadcasted_iota(jnp.int32, shape, len(shape) - 1)


def roll(x, shift):
    return pltpu.roll(x, shift % SEG, x.ndim - 1)


def conv_kernel(pos_ref, low_ref, main_ref, high_ref, edge_ref, w1_ref, w2_ref, out_ref, xs, hid, hs):
    lane = lane_iota((C, SEG))

    def shifted_rows(read, write, edge, rows_of_slot, dilation, first_left, first_right):
        for slot in range(SLOTS):
            low = slot * SLOT_ROWS
            high = low + rows_of_slot(slot)

            def one(row, carry):
                x = read(row)
                tile = edge(row - low)
                left = jnp.where(
                    lane < dilation, roll(tile, -(16 * slot + first_left)), roll(x, dilation)
                )
                right = jnp.where(
                    lane >= SEG - dilation,
                    roll(tile, SEG - dilation - 16 * slot - first_right),
                    roll(x, -dilation),
                )
                write(row, left, x, right)
                return carry

            lax.fori_loop(low, high, one, 0, unroll=3)

    def write_xs(row, left, x, right):
        xs[row, 0:C] = left
        xs[row, C : 2 * C] = x
        xs[row, 2 * C : 3 * C] = right

    def write_hs(row, left, x, right):
        hs[row, 0:C] = left
        hs[row, C : 2 * C] = x
        hs[row, 2 * C : 3 * C] = right

    for row in range(HALO):
        hid[row] = low_ref[0, row]
        hid[ROWS + HALO + row] = high_ref[0, row]

    def fill(row, carry):
        hid[HALO + row] = main_ref[0, row]
        return carry

    lax.fori_loop(0, ROWS, fill, 0, unroll=4)
    shifted_rows(
        lambda row: hid[row],
        write_xs,
        lambda tile: edge_ref[0, tile],
        lambda slot: SLOT_ROWS + (2 * D1 if slot == SLOTS - 1 else 0),
        D1,
        4,
        10,
    )

    def packed(tile, carry):
        x = edge_ref[0, tile]
        write_xs(IMG_ROWS + tile, roll(x, D1), x, roll(x, -D1))
        return carry

    lax.fori_loop(0, EDGE_TILES, packed, 0)

    first_row = pos_ref[0] * ROWS - D2
    height = pos_ref[2]

    def taps(ref, row, step):
        return jnp.concatenate([ref[row], ref[row + step], ref[row + 2 * step]], axis=0)

    def silu(v):
        half = 0.5 * v
        return half + half * jnp.tanh(half)

    def conv1(pair, carry):
        row = 2 * pair
        window = jnp.concatenate([taps(xs, row, D1), taps(xs, row + 1, D1)], axis=1)
        act = silu(jnp.dot(w1_ref[...], window, preferred_element_type=jnp.float32))
        for part in range(2):
            at = first_row + row + part
            inside = ((at >= 0) & (at < height)).astype(jnp.float32)
            hid[row + part] = (act[:, part * SEG : (part + 1) * SEG] * inside).astype(jnp.bfloat16)
        return carry

    lax.fori_loop(0, HID_ROWS // 2, conv1, 0, unroll=2)

    at_left = pos_ref[1] == 0
    at_right = pos_ref[1] == pos_ref[3] - 1
    slot_row = SLOT_ROWS * (lane // 16) + first_row
    is_left = (lane % 16) < 8
    open_side = jnp.where(is_left, jnp.where(at_left, 0.0, 1.0), jnp.where(at_right, 0.0, 1.0))

    def conv1_packed(tile, carry):
        act = silu(
            jnp.dot(
                w1_ref[...], taps(xs, IMG_ROWS + tile, D1), preferred_element_type=jnp.float32
            )
        )
        at = slot_row + tile
        inside = jnp.where((at >= 0) & (at < height), open_side, 0.0)
        hid[HID_ROWS + tile] = (act * inside).astype(jnp.bfloat16)
        return carry

    lax.fori_loop(0, SLOT_ROWS, conv1_packed, 0, unroll=3)

    shifted_rows(
        lambda row: hid[row],
        write_hs,
        lambda tile: hid[HID_ROWS + tile],
        lambda slot: SLOT_ROWS,
        D2,
        2,
        10,
    )

    def conv2(pair, carry):
        row = 2 * pair
        window = jnp.concatenate([taps(hs, row, D2), taps(hs, row + 1, D2)], axis=1)
        total = jnp.dot(w2_ref[...], window, preferred_element_type=jnp.float32)
        base = jnp.concatenate([main_ref[0, row], main_ref[0, row + 1]], axis=1)
        feats = (base.astype(jnp.float32) + total).astype(jnp.bfloat16).astype(jnp.float32)
        scale = lax.rsqrt(jnp.mean(feats * feats, axis=0, keepdims=True) + EPS)
        unit = (feats * scale).astype(jnp.bfloat16)
        out_ref[0, row] = unit[:, :SEG]
        out_ref[0, row + 1] = unit[:, SEG:]
        return carry

    lax.fori_loop(0, ROWS // 2, conv2, 0, unroll=2)


def conv_features(pos, low, main, high, edges, w1, w2):
    count = main.shape[0]
    block = lambda a: pl.BlockSpec((1,) + a.shape[1:], lambda n: (n, 0, 0, 0))
    whole = pl.BlockSpec((C, 9 * C), lambda n: (0, 0))
    return pl.pallas_call(
        conv_kernel,
        grid=(count,),
        in_specs=[
            pl.BlockSpec(memory_space=pltpu.SMEM),
            block(low),
            block(main),
            block(high),
            block(edges),
            whole,
            whole,
        ],
        out_specs=block(main),
        out_shape=jax.ShapeDtypeStruct(main.shape, jnp.bfloat16),
        scratch_shapes=[
            pltpu.VMEM((IMG_ROWS + EDGE_TILES, 3 * C, SEG), jnp.bfloat16),
            pltpu.VMEM((HID_ROWS + SLOT_ROWS, C, SEG), jnp.bfloat16),
            pltpu.VMEM((HID_ROWS, 3 * C, SEG), jnp.bfloat16),
        ],
        compiler_params=pltpu.CompilerParams(vmem_limit_bytes=48 * 1024 * 1024),
        name="features",
    )(pos, low, main, high, edges, w1, w2)


def match_kernel(rng_ref, q_ref, k0_ref, k1_ref, k2_ref, k3_ref, out_ref, disp_ref, keys, qt, acc):
    tri_row = lax.broadcasted_iota(jnp.int32, (SEG, SEG), 0)
    tri_col = lax.broadcasted_iota(jnp.int32, (SEG, SEG), 1)
    lower = tri_row >= tri_col
    scale = SHARP / C * LOG2E

    extra_row = lax.broadcasted_iota(jnp.int32, (16, SEG), 0)
    extra_col = lane_iota((16, SEG)).astype(jnp.float32)

    def fill(block, carry):
        value = jnp.where(
            extra_row == 0,
            1.0,
            jnp.where(extra_row == 1, extra_col, jnp.where(extra_row == 2, block.astype(jnp.float32), 0.0)),
        ).astype(jnp.bfloat16)
        for row in range(RG):
            keys[block, row, C:] = value
        return carry

    lax.fori_loop(0, KEYS + PLANE, fill, 0)
    keys[0, :, :C] = k3_ref[0]

    def fill_keys(block, carry):
        keys[1 + block, :, :C] = k2_ref[block]
        keys[1 + PLANE + block, :, :C] = k1_ref[block]
        keys[1 + 2 * PLANE + block, :, :C] = k0_ref[block]
        return carry

    lax.fori_loop(0, PLANE, fill_keys, 0)

    def values_dot(weights, values):
        return lax.dot_general(
            weights, values, (((1,), (1,)), ((), ())), preferred_element_type=jnp.float32
        )

    def one_block(q, carry):
        least = rng_ref[0, q]
        count = rng_ref[1, q]
        first = KEYS + q - least
        last = first - count
        for row in range(RG):
            qr = q_ref[q, row].T
            qt[row] = qr
            ka = keys[first, row]
            kb = keys[last, row]
            both = jnp.concatenate([ka, kb], axis=1)
            s = jnp.dot(qr, both[:C], preferred_element_type=jnp.float32)
            s = jnp.where(lower, s[:, :SEG], s[:, SEG:])
            w = jnp.exp2(s * scale)
            wide = jnp.concatenate([jnp.where(lower, w, 0.0), jnp.where(lower, 0.0, w)], axis=1)
            acc[row] = values_dot(wide.astype(jnp.bfloat16), both)

        def interior(step, carry):
            at = first - 1 - 2 * step
            for row in range(RG):
                both = jnp.concatenate([keys[at, row], keys[at - 1, row]], axis=1)
                s = jnp.dot(qt[row], both[:C], preferred_element_type=jnp.float32)
                w = jnp.exp2(s * scale).astype(jnp.bfloat16)
                acc[row] += values_dot(w, both)
            return carry

        lax.fori_loop(0, (count - 1) // 2, interior, 0)

        @pl.when((count - 1) % 2 == 1)
        def _():
            for row in range(RG):
                one = keys[last + 1, row]
                s = jnp.dot(qt[row], one[:C], preferred_element_type=jnp.float32)
                w = jnp.exp2(s * scale).astype(jnp.bfloat16)
                acc[row] += values_dot(w, one)

        column = lane_iota((1, SEG)).astype(jnp.float32)
        for row in range(RG):
            t = acc[row].T
            norm = t[C : C + 1]
            inverse = 1.0 / norm
            out_ref[q, row] = (t[:C] * inverse).astype(jnp.bfloat16)
            top = (KEYS + q).astype(jnp.float32)
            hops = top - t[C + 2 : C + 3] * inverse
            within = column - t[C + 1 : C + 2] * inverse
            disp_ref[q, row : row + 1] = hops + within * (1.0 / SEG)
        return carry

    lax.fori_loop(0, PLANE, one_block, 0)


def match(rng, q, k0, k1, k2, k3):
    vmem = pl.BlockSpec(memory_space=pltpu.VMEM)
    return pl.pallas_call(
        match_kernel,
        in_specs=[pl.BlockSpec(memory_space=pltpu.SMEM)] + [vmem] * 5,
        out_specs=(vmem, vmem),
        out_shape=(
            jax.ShapeDtypeStruct((PLANE, RG, C, SEG), jnp.bfloat16),
            jax.ShapeDtypeStruct((PLANE, RG, SEG), jnp.float32),
        ),
        scratch_shapes=[
            pltpu.VMEM((KEYS + PLANE, RG, VROWS, SEG), jnp.bfloat16),
            pltpu.VMEM((RG, SEG, C), jnp.bfloat16),
            pltpu.VMEM((RG, SEG, VROWS), jnp.float32),
        ],
        compiler_params=pltpu.CompilerParams(vmem_limit_bytes=48 * 1024 * 1024),
        name="match",
    )(rng, q, k0, k1, k2, k3)


def shift(value, axis, steps):
    count = lax.axis_size(axis)
    first, last = max(0, -steps), min(count, count - steps)
    return lax.ppermute(value, axis, [(s, s + steps) for s in range(first, last)])


def per_device(images, first_weight, second_weight, search_ranges):
    columns = lax.axis_size("cols")
    groups = [list(range(g, g + PLANE)) for g in range(0, columns, PLANE)]
    flat = lambda w: w.transpose(1, 0, 2).reshape(C, 9 * C)
    w1, w2 = flat(first_weight), flat(second_weight)
    main = images.transpose(0, 2, 1, 3)
    low = shift(main[:, ROWS - HALO :], "rows", 1)
    high = shift(main[:, :HALO], "rows", -1)
    strips = jnp.concatenate([main[..., : HALO], main[..., SEG - HALO :]], axis=-1)
    ends = lambda a: jnp.concatenate([a[..., :HALO], a[..., SEG - HALO :]], axis=-1)
    rows76 = jnp.concatenate([ends(low), strips, ends(high)], axis=1)
    right = shift(rows76[..., HALO:], "cols", 1)
    left = shift(rows76[..., :HALO], "cols", -1)
    slots = jnp.concatenate(
        [right, rows76[..., :2], rows76[..., 2 * HALO - 2 :], left], axis=-1
    )
    tiles = jnp.stack(
        [slots[:, SLOT_ROWS * s : SLOT_ROWS * s + EDGE_TILES] for s in range(SLOTS)], axis=3
    )
    tiles = tiles.reshape(tiles.shape[:3] + (SEG,))
    pos = jnp.stack(
        [
            lax.axis_index("rows"),
            lax.axis_index("cols"),
            ROWS * lax.axis_size("rows"),
            columns,
        ]
    ).astype(jnp.int32)
    unit = conv_features(pos, low, main, high, tiles, w1, w2)

    def spread(a):
        return lax.all_to_all(a, "cols", 0, 0, axis_index_groups=groups, tiled=True)

    rng = lax.all_to_all(search_ranges, "cols", 1, 2, axis_index_groups=groups, tiled=True)[:, 0]
    q = spread(unit[0]).reshape(PLANE, RG, C, SEG)
    k0 = spread(unit[1]).reshape(PLANE, RG, C, SEG)
    k1 = shift(k0, "cols", PLANE)
    k2 = shift(k1, "cols", PLANE)
    k3 = shift(k2[PLANE - 1 :], "cols", PLANE)
    found, disp = match(rng, q, k0, k1, k2, k3)
    matched = spread(found.reshape(PLANE * RG, C, SEG)).transpose(1, 0, 2)
    disparity = spread(disp.reshape(PLANE * RG, SEG))
    return matched, disparity


def solution(mesh):
    placed = (P(None, None, "rows", "cols"), P(), P(), P(None, "rows", "cols"))
    return jax.shard_map(
        per_device,
        mesh=mesh,
        in_specs=placed,
        out_specs=(P(None, "rows", "cols"), P("rows", "cols")),
        check_vma=False,
    )
```

```python
import functools

import jax
import jax.numpy as jnp
from jax import lax
from jax.experimental import pallas as pl
from jax.experimental.pallas import tpu as pltpu
from jax.sharding import PartitionSpec as P

C = 64
SEG = 128
RG = 8
D1 = 2
D2 = 4
EPS = 1e-05
SHARP = 10.0
LOG2E = 1.4426950408889634
ROWS = 64
HALO = D1 + D2
SLOTS = 8
SLOT_ROWS = (ROWS + 2 * D2) // SLOTS
EDGE_TILES = SLOT_ROWS + 2 * D1
IMG_ROWS = ROWS + 2 * HALO
HID_ROWS = ROWS + 2 * D2
PLANE = 8
KEYS = 2 * PLANE + 1
MESH = pl.DeviceIdType.MESH
VROWS = 80


def lane_iota(shape):
    return lax.broadcasted_iota(jnp.int32, shape, len(shape) - 1)


def roll(x, shift):
    return pltpu.roll(x, shift % SEG, x.ndim - 1)


def features_kernel(
    images, w1_ref, w2_ref, q_out, k_out,
    img, edge, from_left, from_right, xs, hid, hs, unit, w1, w2,
    load_sem, row_send, row_recv, col_send, col_recv,
    spread_send, spread_recv, near_send, near_recv, far_send, far_recv, last_send, last_recv, own_sem,
):
    row_count, col_count = lax.axis_size("rows"), lax.axis_size("cols")
    x, col = lax.axis_index("rows"), lax.axis_index("cols")
    me = lax.rem(col, PLANE)
    base = col - me
    lane = lane_iota((C, SEG))

    def at_row(step):
        return (lax.rem(x + step + row_count, row_count), col)

    def at_col(step):
        return (x, lax.rem(col + step + col_count, col_count))

    barrier = pltpu.get_barrier_semaphore()
    friends = [at_row(1), at_row(-1), at_col(1), at_col(-1), at_col(PLANE), at_col(-PLANE)]
    friends += [(x, base + lax.rem(me + o, PLANE)) for o in range(1, PLANE)]
    for friend in friends:
        pl.semaphore_signal(barrier, inc=1, device_id=friend, device_id_type=MESH)

    loads = [
        pltpu.make_async_copy(images.at[n], img.at[n, pl.ds(HALO, ROWS)], load_sem.at[n])
        for n in range(2)
    ]
    loads[1].start()
    loads[0].start()
    pl.semaphore_wait(barrier, len(friends))

    def remote(src, dst, send, recv, device):
        return pltpu.make_async_remote_copy(
            src_ref=src, dst_ref=dst, send_sem=send, recv_sem=recv,
            device_id=device, device_id_type=MESH,
        )

    row_copies = {}
    for n in (1, 0):
        down = remote(
            images.at[n, pl.ds(ROWS - HALO, HALO)], img.at[n, pl.ds(0, HALO)],
            row_send.at[n, 0], row_recv.at[n, 0], at_row(1),
        )
        up = remote(
            images.at[n, pl.ds(0, HALO)], img.at[n, pl.ds(HALO + ROWS, HALO)],
            row_send.at[n, 1], row_recv.at[n, 1], at_row(-1),
        )
        down.start()
        up.start()
        row_copies[n] = (down, up)

    for ref, out in ((w1_ref, w1), (w2_ref, w2)):
        taps = jnp.concatenate([ref[t] for t in range(9)], axis=1)
        none = jnp.zeros((C, 3 * C), jnp.bfloat16)
        out[0:C] = jnp.concatenate([taps, none], axis=1)
        out[C:] = jnp.concatenate([none, taps], axis=1)

    col_copies = {}
    for n in (1, 0):
        loads[n].wait()
        for copy in row_copies[n]:
            copy.wait()

        @pl.when(x == 0)
        def _(n=n):
            img[n, 0:HALO] = jnp.zeros((HALO, C, SEG), jnp.bfloat16)

        @pl.when(x == row_count - 1)
        def _(n=n):
            img[n, HALO + ROWS :] = jnp.zeros((HALO, C, SEG), jnp.bfloat16)

        def pack(tile, carry, n=n):
            packed = jnp.zeros((C, SEG), jnp.bfloat16)
            for slot in range(SLOTS):
                row = img[n, SLOT_ROWS * slot + tile]
                start = 16 * slot
                packed = jnp.where((lane >= start) & (lane < start + 8), roll(row, start + 6), packed)
                packed = jnp.where((lane >= start + 8) & (lane < start + 16), roll(row, start + 10), packed)
            edge[n, tile] = packed
            return carry

        lax.fori_loop(0, EDGE_TILES, pack, 0)
        right = remote(edge.at[n], from_left.at[n], col_send.at[n, 0], col_recv.at[n, 0], at_col(1))
        left = remote(edge.at[n], from_right.at[n], col_send.at[n, 1], col_recv.at[n, 1], at_col(-1))
        right.start()
        left.start()
        col_copies[n] = (right, left)

    part = lane % 16
    inner = (part >= 6) & (part < 10)
    low_part = part < 6
    left_open = jnp.where(col == 0, 0.0, 1.0)
    right_open = jnp.where(col == col_count - 1, 0.0, 1.0)
    open_side = jnp.where(part < 8, left_open, right_open)
    first_row = x * ROWS - D2
    height = row_count * ROWS
    slot_row = SLOT_ROWS * (lane // 16) + first_row

    def shifted(read, edges, rows, dest, dilation, first_left, first_right):
        for slot in range(SLOTS):
            low = slot * SLOT_ROWS
            high = rows if slot == SLOTS - 1 else low + SLOT_ROWS

            def one(row, carry, slot=slot, low=low):
                value = read(row)
                tile = edges(row - low)
                dest[row, 0:C] = jnp.where(
                    lane < dilation, roll(tile, -(16 * slot + first_left)), roll(value, dilation)
                )
                dest[row, C : 2 * C] = value
                dest[row, 2 * C :] = jnp.where(
                    lane >= SEG - dilation,
                    roll(tile, SEG - dilation - 16 * slot - first_right),
                    roll(value, -dilation),
                )
                return carry

            lax.fori_loop(low, high, one, 0, unroll=3)

    def window(ref, row, step, count):
        return jnp.concatenate([ref[row + step * t] for t in range(count)], axis=0)

    def four(weights, ref, row, step):
        both = jnp.concatenate([window(ref, row, step, 4), window(ref, row + 1, step, 4)], axis=1)
        return jnp.dot(weights[...], both, preferred_element_type=jnp.float32)

    def silu(v):
        half = 0.5 * v
        return half + half * jnp.tanh(half)

    def spread(n, group):
        out = k_out.at[2 * PLANE + 1 + me] if n else q_out.at[me]
        return remote(
            unit.at[n, pl.ds(RG * group, RG)], out,
            spread_send.at[n, group], spread_recv.at[n, me], (x, base + group),
        )

    def arrived(n, source):
        out = k_out.at[2 * PLANE + 1 + source] if n else q_out.at[source]
        remote(
            unit.at[n, pl.ds(RG * source, RG)], out,
            spread_send.at[n, source], spread_recv.at[n, source], (x, base + source),
        ).wait_recv()

    def convolve(n, between):
        for copy in col_copies[n]:
            copy.wait()

        def merge(tile, carry):
            ours = edge[n, tile]
            left = from_left[n, tile] * left_open.astype(jnp.bfloat16)
            right = from_right[n, tile] * right_open.astype(jnp.bfloat16)
            value = jnp.where(inner, ours, jnp.where(low_part, left, right))
            edge[n, tile] = value
            dest = IMG_ROWS + tile
            xs[dest, 0:C] = roll(value, D1)
            xs[dest, C : 2 * C] = value
            xs[dest, 2 * C :] = roll(value, -D1)
            return carry

        lax.fori_loop(0, EDGE_TILES, merge, 0)
        shifted(lambda row: img[n, row], lambda t: edge[n, t], IMG_ROWS, xs, D1, 4, 10)
        between(0)

        def conv1(step, carry):
            row = 4 * step
            act = silu(four(w1, xs, row, D1))
            for a in range(2):
                for b in range(2):
                    at = first_row + row + 2 * a + b
                    inside = jnp.where((at >= 0) & (at < height), 1.0, 0.0)
                    value = act[C * a : C * (a + 1), SEG * b : SEG * (b + 1)]
                    hid[row + 2 * a + b] = (value * inside).astype(jnp.bfloat16)
            return carry

        lax.fori_loop(0, HID_ROWS // 4, conv1, 0, unroll=2)

        def packed_hidden(tile, act):
            at = slot_row + tile
            inside = jnp.where((at >= 0) & (at < height), open_side, 0.0)
            hid[HID_ROWS + tile] = (act * inside).astype(jnp.bfloat16)

        def conv1_packed(step, carry):
            tile = 4 * step
            act = silu(four(w1, xs, IMG_ROWS + tile, D1))
            for a in range(2):
                for b in range(2):
                    value = act[C * a : C * (a + 1), SEG * b : SEG * (b + 1)]
                    packed_hidden(tile + 2 * a + b, value)
            return carry

        lax.fori_loop(0, SLOT_ROWS // 4, conv1_packed, 0, unroll=2)
        tile = SLOT_ROWS - 1
        end = window(xs, IMG_ROWS + tile, D1, 3)
        packed_hidden(tile, silu(jnp.dot(w1[0:C, 0 : 9 * C], end, preferred_element_type=jnp.float32)))
        between(1)
        shifted(lambda row: hid[row], lambda t: hid[HID_ROWS + t], HID_ROWS, hs, D2, 2, 10)
        between(2)

        def conv2(group, carry):
            for half in range(2):
                row = RG * group + 2 * half
                total = four(w2, hs, row, D2)
                for a in range(2):
                    for b in range(2):
                        at = row + 4 * a + b
                        value = total[C * a : C * (a + 1), SEG * b : SEG * (b + 1)]
                        feats = (img[n, HALO + at].astype(jnp.float32) + value).astype(jnp.bfloat16)
                        feats = feats.astype(jnp.float32)
                        scale = lax.rsqrt(jnp.mean(feats * feats, axis=0, keepdims=True) + EPS)
                        unit[n, at] = (feats * scale).astype(jnp.bfloat16)

            @pl.when(group != me)
            def _():
                spread(n, group).start()

            return carry

        lax.fori_loop(0, PLANE, conv2, 0)

    convolve(1, lambda stage: None)

    own_k = pltpu.make_async_copy(
        unit.at[1, pl.ds(RG * me, RG)], k_out.at[2 * PLANE + 1 + me], own_sem.at[1]
    )
    own_k.start()

    def near(block, src):
        return remote(
            src, k_out.at[PLANE + 1 + block], near_send.at[block], near_recv.at[block], at_col(PLANE)
        )

    def far(block):
        return remote(
            k_out.at[PLANE + 1 + block], k_out.at[1 + block],
            far_send.at[block], far_recv.at[block], at_col(PLANE),
        )

    last = remote(k_out.at[PLANE], k_out.at[0], last_send, last_recv, at_col(PLANE))
    near(me, unit.at[1, pl.ds(RG * me, RG)]).start()

    def block_of(o):
        return lax.rem(me + o, PLANE)

    def forward(offsets):
        for o in offsets:
            block = block_of(o)
            arrived(1, block)
            near(block, k_out.at[2 * PLANE + 1 + block]).start()

    convolve(0, lambda stage: forward(((1, 2), (3, 4), (5, 6, 7))[stage]))
    own_q = pltpu.make_async_copy(unit.at[0, pl.ds(RG * me, RG)], q_out.at[me], own_sem.at[0])
    own_q.start()

    def relay(o, carry):
        block = block_of(o)
        near(block, k_out.at[2 * PLANE + 1 + block]).wait_recv()
        far(block).start()
        return carry

    lax.fori_loop(0, PLANE, relay, 0)

    def collect(o, carry):
        far(block_of(o)).wait_recv()
        return carry

    lax.fori_loop(0, PLANE, collect, 0)
    last.start()

    def finish(o, carry):
        block = block_of(o)
        arrived(0, block)
        for n in range(2):
            spread(n, block).wait_send()
        return carry

    lax.fori_loop(1, PLANE, finish, 0)

    def sent(block, carry):
        near(block, k_out.at[2 * PLANE + 1 + block]).wait_send()
        far(block).wait_send()
        return carry

    lax.fori_loop(0, PLANE, sent, 0)
    own_k.wait()
    own_q.wait()
    last.wait()


def features(images, w1, w2):
    anywhere = pl.BlockSpec(memory_space=pl.ANY)
    vmem = pl.BlockSpec(memory_space=pltpu.VMEM)
    dma = pltpu.SemaphoreType.DMA
    bf16 = jnp.bfloat16
    return pl.pallas_call(
        features_kernel,
        in_specs=[anywhere, vmem, vmem],
        out_specs=(anywhere, anywhere),
        out_shape=(
            jax.ShapeDtypeStruct((PLANE, RG, C, SEG), bf16),
            jax.ShapeDtypeStruct((KEYS + PLANE, RG, C, SEG), bf16),
        ),
        scratch_shapes=[
            pltpu.VMEM((2, IMG_ROWS, C, SEG), bf16),
            pltpu.VMEM((2, EDGE_TILES, C, SEG), bf16),
            pltpu.VMEM((2, EDGE_TILES, C, SEG), bf16),
            pltpu.VMEM((2, EDGE_TILES, C, SEG), bf16),
            pltpu.VMEM((IMG_ROWS + EDGE_TILES, 3 * C, SEG), bf16),
            pltpu.VMEM((HID_ROWS + SLOT_ROWS, C, SEG), bf16),
            pltpu.VMEM((HID_ROWS, 3 * C, SEG), bf16),
            pltpu.VMEM((2, ROWS, C, SEG), bf16),
            pltpu.VMEM((2 * C, 12 * C), bf16),
            pltpu.VMEM((2 * C, 12 * C), bf16),
            dma((2,)), dma((2, 2)), dma((2, 2)), dma((2, 2)), dma((2, 2)),
            dma((2, PLANE)), dma((2, PLANE)),
            dma((PLANE,)), dma((PLANE,)), dma((PLANE,)), dma((PLANE,)),
            dma, dma, dma((2,)),
        ],
        compiler_params=pltpu.CompilerParams(
            collective_id=0, has_side_effects=True, vmem_limit_bytes=48 * 1024 * 1024
        ),
        name="features",
    )(images, w1, w2)


def match_kernel(rng_ref, q_ref, k_ref, out_ref, disp_ref, keys, qt, acc):
    tri_row = lax.broadcasted_iota(jnp.int32, (SEG, SEG), 0)
    tri_col = lax.broadcasted_iota(jnp.int32, (SEG, SEG), 1)
    lower = tri_row >= tri_col
    scale = SHARP / C * LOG2E

    extra_row = lax.broadcasted_iota(jnp.int32, (16, SEG), 0)
    extra_col = lane_iota((16, SEG)).astype(jnp.float32)

    def fill(block, carry):
        value = jnp.where(
            extra_row == 0,
            1.0,
            jnp.where(extra_row == 1, extra_col, jnp.where(extra_row == 2, block.astype(jnp.float32), 0.0)),
        ).astype(jnp.bfloat16)
        for row in range(RG):
            keys[block, row, C:] = value
        return carry

    lax.fori_loop(0, KEYS + PLANE, fill, 0)

    absent = jnp.maximum(KEYS - PLANE * rng_ref[2, 0], 0)

    def fill_keys(block, carry):
        keys[block, :, :C] = k_ref[block]
        return carry

    def clear_keys(block, carry):
        keys[block, :, :C] = jnp.zeros((RG, C, SEG), jnp.bfloat16)
        return carry

    lax.fori_loop(0, absent, clear_keys, 0)
    lax.fori_loop(absent, KEYS + PLANE, fill_keys, 0)

    def values_dot(weights, values):
        return lax.dot_general(
            weights, values, (((1,), (1,)), ((), ())), preferred_element_type=jnp.float32
        )

    def one_block(q, carry):
        least = rng_ref[0, q]
        count = rng_ref[1, q]
        first = KEYS + q - least
        last = first - count
        for row in range(RG):
            qr = q_ref[q, row].T
            qt[row] = qr
            ka = keys[first, row]
            kb = keys[last, row]
            both = jnp.concatenate([ka, kb], axis=1)
            s = jnp.dot(qr, both[:C], preferred_element_type=jnp.float32)
            s = jnp.where(lower, s[:, :SEG], s[:, SEG:])
            w = jnp.exp2(s * scale)
            wide = jnp.concatenate([jnp.where(lower, w, 0.0), jnp.where(lower, 0.0, w)], axis=1)
            acc[row] = values_dot(wide.astype(jnp.bfloat16), both)

        def interior(step, carry):
            at = first - 1 - 2 * step
            for row in range(RG):
                both = jnp.concatenate([keys[at, row], keys[at - 1, row]], axis=1)
                s = jnp.dot(qt[row], both[:C], preferred_element_type=jnp.float32)
                w = jnp.exp2(s * scale).astype(jnp.bfloat16)
                acc[row] += values_dot(w, both)
            return carry

        lax.fori_loop(0, (count - 1) // 2, interior, 0)

        @pl.when((count - 1) % 2 == 1)
        def _():
            for row in range(RG):
                one = keys[last + 1, row]
                s = jnp.dot(qt[row], one[:C], preferred_element_type=jnp.float32)
                w = jnp.exp2(s * scale).astype(jnp.bfloat16)
                acc[row] += values_dot(w, one)

        column = lane_iota((1, SEG)).astype(jnp.float32)
        for row in range(RG):
            t = acc[row].T
            norm = t[C : C + 1]
            inverse = 1.0 / norm
            out_ref[q, row] = (t[:C] * inverse).astype(jnp.bfloat16)
            top = (KEYS + q).astype(jnp.float32)
            hops = top - t[C + 2 : C + 3] * inverse
            within = column - t[C + 1 : C + 2] * inverse
            disp_ref[q, row : row + 1] = hops + within * (1.0 / SEG)
        return carry

    lax.fori_loop(0, PLANE, one_block, 0)


def match(rng, q, keys):
    vmem = pl.BlockSpec(memory_space=pltpu.VMEM)
    return pl.pallas_call(
        match_kernel,
        in_specs=[pl.BlockSpec(memory_space=pltpu.SMEM)] + [vmem] * 2,
        out_specs=(vmem, vmem),
        out_shape=(
            jax.ShapeDtypeStruct((PLANE, RG, C, SEG), jnp.bfloat16),
            jax.ShapeDtypeStruct((PLANE, RG, SEG), jnp.float32),
        ),
        scratch_shapes=[
            pltpu.VMEM((KEYS + PLANE, RG, VROWS, SEG), jnp.bfloat16),
            pltpu.VMEM((RG, SEG, C), jnp.bfloat16),
            pltpu.VMEM((RG, SEG, VROWS), jnp.float32),
        ],
        compiler_params=pltpu.CompilerParams(vmem_limit_bytes=48 * 1024 * 1024),
        name="match",
    )(rng, q, keys)


def return_kernel(found, disp, found_out, disp_out, found_send, found_recv, disp_send, disp_recv, own_sem):
    x, col = lax.axis_index("rows"), lax.axis_index("cols")
    me = lax.rem(col, PLANE)
    base = col - me
    peers = [lax.rem(me + o, PLANE) for o in range(1, PLANE)]
    barrier = pltpu.get_barrier_semaphore()
    for peer in peers:
        pl.semaphore_signal(barrier, inc=1, device_id=(x, base + peer), device_id_type=MESH)
    own = [
        pltpu.make_async_copy(found.at[me], found_out.at[me], own_sem.at[0]),
        pltpu.make_async_copy(disp.at[me], disp_out.at[me], own_sem.at[1]),
    ]
    for copy in own:
        copy.start()
    pl.semaphore_wait(barrier, len(peers))

    def both(peer, slot):
        return [
            pltpu.make_async_remote_copy(
                src_ref=src.at[peer], dst_ref=dst.at[slot], send_sem=send.at[peer],
                recv_sem=recv.at[slot], device_id=(x, base + peer), device_id_type=MESH,
            )
            for src, dst, send, recv in (
                (found, found_out, found_send, found_recv),
                (disp, disp_out, disp_send, disp_recv),
            )
        ]

    for peer in peers:
        for copy in both(peer, me):
            copy.start()
    for peer in peers:
        for copy in both(peer, peer):
            copy.wait_send()
            copy.wait_recv()
    for copy in own:
        copy.wait()


def give_back(found, disp):
    anywhere = pl.BlockSpec(memory_space=pl.ANY)
    dma = pltpu.SemaphoreType.DMA
    return pl.pallas_call(
        return_kernel,
        in_specs=[anywhere, anywhere],
        out_specs=(anywhere, anywhere),
        out_shape=(
            jax.ShapeDtypeStruct(found.shape, found.dtype),
            jax.ShapeDtypeStruct(disp.shape, disp.dtype),
        ),
        scratch_shapes=[dma((PLANE,))] * 4 + [dma((2,))],
        compiler_params=pltpu.CompilerParams(collective_id=1, has_side_effects=True),
        name="give_back",
    )(found, disp)


def per_device(images, first_weight, second_weight, search_ranges):
    columns = lax.axis_size("cols")
    groups = [list(range(g, g + PLANE)) for g in range(0, columns, PLANE)]
    ranges = lax.all_to_all(search_ranges, "cols", 1, 2, axis_index_groups=groups, tiled=True)
    plane = jnp.full((1, PLANE), lax.axis_index("cols") // PLANE, jnp.int32)
    ranges = jnp.concatenate([ranges[:, 0], plane], axis=0)
    q, keys = features(images.transpose(0, 2, 1, 3), first_weight, second_weight)
    found, disp = match(ranges, q, keys)
    matched, disparity = give_back(found, disp)
    return (
        matched.reshape(ROWS, C, SEG).transpose(1, 0, 2),
        disparity.reshape(ROWS, SEG),
    )


def solution(mesh):
    placed = (P(None, None, "rows", "cols"), P(), P(), P(None, "rows", "cols"))
    return jax.shard_map(
        per_device,
        mesh=mesh,
        in_specs=placed,
        out_specs=(P(None, "rows", "cols"), P("rows", "cols")),
        check_vma=False,
    )
```

```python
import functools

import jax
import jax.numpy as jnp
from jax import lax
from jax.experimental import pallas as pl
from jax.experimental.pallas import tpu as pltpu
from jax.sharding import PartitionSpec as P

C = 64
SEG = 128
RG = 8
D1 = 2
D2 = 4
EPS = 1e-05
SHARP = 10.0
LOG2E = 1.4426950408889634
ROWS = 64
HALO = D1 + D2
SLOTS = 8
SLOT_ROWS = (ROWS + 2 * D2) // SLOTS
EDGE_TILES = SLOT_ROWS + 2 * D1
IMG_ROWS = ROWS + 2 * HALO
HID_ROWS = ROWS + 2 * D2
PLANE = 8
KEYS = 2 * PLANE + 1
MESH = pl.DeviceIdType.MESH
VROWS = 80


def lane_iota(shape):
    return lax.broadcasted_iota(jnp.int32, shape, len(shape) - 1)


def roll(x, shift):
    return pltpu.roll(x, shift % SEG, x.ndim - 1)


def features_kernel(
    ranges, images, w1_ref, w2_ref, found_out, disp_out,
    img, edge, from_left, from_right, xs, hid, hs, unit, w1, w2,
    queries, keys, acc, bias, found, disp, range_tiles, range_all,
    load_sem, row_send, row_recv, col_send, col_recv,
    spread_send, spread_recv, near_send, near_recv, far_send, far_recv, last_send, last_recv, own_sem,
    range_send, range_recv, found_send, found_recv, disp_send, disp_recv,
):
    row_count, col_count = lax.axis_size("rows"), lax.axis_size("cols")
    x, col = lax.axis_index("rows"), lax.axis_index("cols")
    me = lax.rem(col, PLANE)
    base = col - me
    lane = lane_iota((C, SEG))

    def at_row(step):
        return (lax.rem(x + step + row_count, row_count), col)

    def at_col(step):
        return (x, lax.rem(col + step + col_count, col_count))

    barrier = pltpu.get_barrier_semaphore()
    friends = [at_row(1), at_row(-1), at_col(1), at_col(-1), at_col(PLANE), at_col(-PLANE)]
    friends += [(x, base + lax.rem(me + o, PLANE)) for o in range(1, PLANE)]
    for friend in friends:
        pl.semaphore_signal(barrier, inc=1, device_id=friend, device_id_type=MESH)

    loads = [
        pltpu.make_async_copy(images.at[n], img.at[n, pl.ds(HALO, ROWS)], load_sem.at[n])
        for n in range(2)
    ]
    loads[1].start()
    loads[0].start()
    pl.semaphore_wait(barrier, len(friends))

    def remote(src, dst, send, recv, device):
        return pltpu.make_async_remote_copy(
            src_ref=src, dst_ref=dst, send_sem=send, recv_sem=recv,
            device_id=device, device_id_type=MESH,
        )

    row_copies = {}
    for n in (1, 0):
        down = remote(
            images.at[n, pl.ds(ROWS - HALO, HALO)], img.at[n, pl.ds(0, HALO)],
            row_send.at[n, 0], row_recv.at[n, 0], at_row(1),
        )
        up = remote(
            images.at[n, pl.ds(0, HALO)], img.at[n, pl.ds(HALO + ROWS, HALO)],
            row_send.at[n, 1], row_recv.at[n, 1], at_row(-1),
        )
        down.start()
        up.start()
        row_copies[n] = (down, up)

    for group in range(PLANE):
        tile_row = lax.broadcasted_iota(jnp.int32, (8, SEG), 0)
        range_tiles[group] = jnp.where(tile_row == 0, ranges[0, group], ranges[1, group])

    def send_range(peer, slot):
        return remote(
            range_tiles.at[peer], range_all.at[slot],
            range_send.at[peer], range_recv.at[slot], (x, base + peer),
        )

    def start_range(o, carry):
        send_range(lax.rem(me + o, PLANE), me).start()
        return carry

    lax.fori_loop(1, PLANE, start_range, 0)
    range_all[me] = range_tiles[me]

    for ref, out in ((w1_ref, w1), (w2_ref, w2)):
        taps = jnp.concatenate([ref[t] for t in range(9)], axis=1)
        none = jnp.zeros((C, 3 * C), jnp.bfloat16)
        out[0:C] = jnp.concatenate([taps, none], axis=1)
        out[C:] = jnp.concatenate([none, taps], axis=1)

    col_copies = {}
    for n in (1, 0):
        loads[n].wait()
        for copy in row_copies[n]:
            copy.wait()

        @pl.when(x == 0)
        def _(n=n):
            img[n, 0:HALO] = jnp.zeros((HALO, C, SEG), jnp.bfloat16)

        @pl.when(x == row_count - 1)
        def _(n=n):
            img[n, HALO + ROWS :] = jnp.zeros((HALO, C, SEG), jnp.bfloat16)

        def pack(tile, carry, n=n):
            packed = jnp.zeros((C, SEG), jnp.bfloat16)
            for slot in range(SLOTS):
                row = img[n, SLOT_ROWS * slot + tile]
                start = 16 * slot
                packed = jnp.where((lane >= start) & (lane < start + 8), roll(row, start + 6), packed)
                packed = jnp.where((lane >= start + 8) & (lane < start + 16), roll(row, start + 10), packed)
            edge[n, tile] = packed
            return carry

        lax.fori_loop(0, EDGE_TILES, pack, 0)
        right = remote(edge.at[n], from_left.at[n], col_send.at[n, 0], col_recv.at[n, 0], at_col(1))
        left = remote(edge.at[n], from_right.at[n], col_send.at[n, 1], col_recv.at[n, 1], at_col(-1))
        right.start()
        left.start()
        col_copies[n] = (right, left)

    part = lane % 16
    inner = (part >= 6) & (part < 10)
    low_part = part < 6
    left_open = jnp.where(col == 0, 0.0, 1.0)
    right_open = jnp.where(col == col_count - 1, 0.0, 1.0)
    open_side = jnp.where(part < 8, left_open, right_open)
    first_row = x * ROWS - D2
    height = row_count * ROWS
    slot_row = SLOT_ROWS * (lane // 16) + first_row

    def shifted(read, edges, rows, dest, dilation, first_left, first_right):
        for slot in range(SLOTS):
            low = slot * SLOT_ROWS
            high = rows if slot == SLOTS - 1 else low + SLOT_ROWS

            def one(row, carry, slot=slot, low=low):
                value = read(row)
                tile = edges(row - low)
                dest[row, 0:C] = jnp.where(
                    lane < dilation, roll(tile, -(16 * slot + first_left)), roll(value, dilation)
                )
                dest[row, C : 2 * C] = value
                dest[row, 2 * C :] = jnp.where(
                    lane >= SEG - dilation,
                    roll(tile, SEG - dilation - 16 * slot - first_right),
                    roll(value, -dilation),
                )
                return carry

            lax.fori_loop(low, high, one, 0, unroll=3)

    def window(ref, row, step, count):
        return jnp.concatenate([ref[row + step * t] for t in range(count)], axis=0)

    def four(weights, ref, row, step):
        both = jnp.concatenate([window(ref, row, step, 4), window(ref, row + 1, step, 4)], axis=1)
        return jnp.dot(weights[...], both, preferred_element_type=jnp.float32)

    def silu(v):
        half = 0.5 * v
        return half + half * jnp.tanh(half)

    def spread(n, group):
        out = keys.at[2 * PLANE + 1 + me] if n else queries.at[me]
        return remote(
            unit.at[n, pl.ds(RG * group, RG)], out,
            spread_send.at[n, group], spread_recv.at[n, me], (x, base + group),
        )

    def arrived(n, source):
        out = keys.at[2 * PLANE + 1 + source] if n else queries.at[source]
        remote(
            unit.at[n, pl.ds(RG * source, RG)], out,
            spread_send.at[n, source], spread_recv.at[n, source], (x, base + source),
        ).wait_recv()

    def convolve(n, between):
        for copy in col_copies[n]:
            copy.wait()

        def merge(tile, carry):
            ours = edge[n, tile]
            left = from_left[n, tile] * left_open.astype(jnp.bfloat16)
            right = from_right[n, tile] * right_open.astype(jnp.bfloat16)
            value = jnp.where(inner, ours, jnp.where(low_part, left, right))
            edge[n, tile] = value
            dest = IMG_ROWS + tile
            xs[dest, 0:C] = roll(value, D1)
            xs[dest, C : 2 * C] = value
            xs[dest, 2 * C :] = roll(value, -D1)
            return carry

        lax.fori_loop(0, EDGE_TILES, merge, 0)
        shifted(lambda row: img[n, row], lambda t: edge[n, t], IMG_ROWS, xs, D1, 4, 10)
        between(0)

        def conv1(step, carry):
            row = 4 * step
            act = silu(four(w1, xs, row, D1))
            for a in range(2):
                for b in range(2):
                    at = first_row + row + 2 * a + b
                    inside = jnp.where((at >= 0) & (at < height), 1.0, 0.0)
                    value = act[C * a : C * (a + 1), SEG * b : SEG * (b + 1)]
                    hid[row + 2 * a + b] = (value * inside).astype(jnp.bfloat16)
            return carry

        lax.fori_loop(0, HID_ROWS // 4, conv1, 0, unroll=2)

        def packed_hidden(tile, act):
            at = slot_row + tile
            inside = jnp.where((at >= 0) & (at < height), open_side, 0.0)
            hid[HID_ROWS + tile] = (act * inside).astype(jnp.bfloat16)

        def conv1_packed(step, carry):
            tile = 4 * step
            act = silu(four(w1, xs, IMG_ROWS + tile, D1))
            for a in range(2):
                for b in range(2):
                    value = act[C * a : C * (a + 1), SEG * b : SEG * (b + 1)]
                    packed_hidden(tile + 2 * a + b, value)
            return carry

        lax.fori_loop(0, SLOT_ROWS // 4, conv1_packed, 0, unroll=2)
        tile = SLOT_ROWS - 1
        end = window(xs, IMG_ROWS + tile, D1, 3)
        packed_hidden(tile, silu(jnp.dot(w1[0:C, 0 : 9 * C], end, preferred_element_type=jnp.float32)))
        between(1)
        shifted(lambda row: hid[row], lambda t: hid[HID_ROWS + t], HID_ROWS, hs, D2, 2, 10)
        between(2)

        def conv2(group, carry):
            for half in range(2):
                row = RG * group + 2 * half
                total = four(w2, hs, row, D2)
                for a in range(2):
                    for b in range(2):
                        at = row + 4 * a + b
                        value = total[C * a : C * (a + 1), SEG * b : SEG * (b + 1)]
                        feats = (img[n, HALO + at].astype(jnp.float32) + value).astype(jnp.bfloat16)
                        feats = feats.astype(jnp.float32)
                        scale = lax.rsqrt(jnp.mean(feats * feats, axis=0, keepdims=True) + EPS)
                        unit[n, at] = (feats * scale).astype(jnp.bfloat16)

            @pl.when(group != me)
            def _():
                spread(n, group).start()

            return carry

        lax.fori_loop(0, PLANE, conv2, 0)

    convolve(1, lambda stage: None)

    own_k = pltpu.make_async_copy(
        unit.at[1, pl.ds(RG * me, RG)], keys.at[2 * PLANE + 1 + me], own_sem.at[1]
    )
    own_k.start()

    def near(block, src):
        return remote(
            src, keys.at[PLANE + 1 + block], near_send.at[block], near_recv.at[block], at_col(PLANE)
        )

    def far(block):
        return remote(
            keys.at[PLANE + 1 + block], keys.at[1 + block],
            far_send.at[block], far_recv.at[block], at_col(PLANE),
        )

    last = remote(keys.at[PLANE], keys.at[0], last_send, last_recv, at_col(PLANE))
    near(me, unit.at[1, pl.ds(RG * me, RG)]).start()

    def block_of(o):
        return lax.rem(me + o, PLANE)

    def forward(blocks):
        for block in blocks:

            @pl.when(block != me)
            def _(block=block):
                arrived(1, block)
                near(block, keys.at[2 * PLANE + 1 + block]).start()

    def relay(blocks):
        for block in blocks:
            near(block, keys.at[2 * PLANE + 1 + block]).wait_recv()
            far(block).start()

    convolve(0, lambda stage: forward(((7, 6, 5), (4, 3, 2), (1, 0))[stage]))
    relay((7, 6, 5))
    own_q = pltpu.make_async_copy(unit.at[0, pl.ds(RG * me, RG)], queries.at[me], own_sem.at[0])
    own_q.start()

    def finish_spread(o, carry):
        block = block_of(o)
        arrived(0, block)
        send_range(block, block).wait_recv()
        send_range(block, block).wait_send()
        for n in range(2):
            spread(n, block).wait_send()
        return carry

    lax.fori_loop(1, PLANE, finish_spread, 0)
    own_k.wait()
    own_q.wait()

    scale = SHARP / C * LOG2E
    plane = col // PLANE
    top = 2 * PLANE + 1

    def attend(first_key, key_blocks, first_q, q_blocks, needed, fresh):
        width, depth = q_blocks * SEG, key_blocks * SEG
        span = pl.ds(first_q * SEG, width)
        within = lane_iota((1, SEG))
        upper = jnp.concatenate(
            [SEG * (top + q - range_all[q, 0:1]) + within for q in range(first_q, first_q + q_blocks)],
            axis=1,
        )
        lower = jnp.concatenate(
            [
                SEG * (top + q - range_all[q, 0:1] - range_all[q, 1:2]) + within
                for q in range(first_q, first_q + q_blocks)
            ],
            axis=1,
        )

        def mask(step, carry):
            at = 64 * step
            key = SEG * first_key + at + lax.broadcasted_iota(jnp.int32, (64, width), 0)
            inside = (key <= upper) & (key > lower)
            bias[pl.ds(pl.multiple_of(at, 64), 64), 0:width] = jnp.where(inside, 0.0, -1e30)
            return carry

        lax.fori_loop(0, depth // 64, mask, 0)
        present = jnp.where(plane >= needed, 1.0, 0.0).astype(jnp.bfloat16)
        extra_row = lax.broadcasted_iota(jnp.int32, (16, SEG), 0)
        column = lane_iota((16, SEG)).astype(jnp.float32)
        extra = jnp.concatenate(
            [
                jnp.where(
                    extra_row == 0,
                    1.0,
                    jnp.where(extra_row == 1, column, jnp.where(extra_row == 2, float(first_key + b), 0.0)),
                )
                for b in range(key_blocks)
            ],
            axis=1,
        ).astype(jnp.bfloat16)

        def one_row(row, carry):
            chunk = jnp.concatenate([keys[first_key + b, row] for b in range(key_blocks)], axis=1)
            if needed:
                chunk = chunk * present
            q = jnp.concatenate([queries[first_q + b, row] for b in range(q_blocks)], axis=1)
            s = jnp.dot(chunk.T, q, preferred_element_type=jnp.float32)
            p = jnp.exp2(s * scale + bias[0:depth, 0:width]).astype(jnp.bfloat16)
            values = jnp.concatenate([chunk, extra], axis=0)
            total = jnp.dot(values, p, preferred_element_type=jnp.float32)
            if fresh:
                acc[row, :, span] = total
            else:
                acc[row, :, span] += total
            return carry

        lax.fori_loop(0, RG, one_row, 0, unroll=2)

    def give_back(peer, slot):
        return [
            remote(
                found.at[peer], found_out.at[slot],
                found_send.at[peer], found_recv.at[slot], (x, base + peer),
            ),
            remote(
                disp.at[peer], disp_out.at[slot],
                disp_send.at[peer], disp_recv.at[slot], (x, base + peer),
            ),
        ]

    def keep(slot):
        return [
            pltpu.make_async_copy(found.at[slot], found_out.at[slot], own_sem.at[2]),
            pltpu.make_async_copy(disp.at[slot], disp_out.at[slot], own_sem.at[3]),
        ]

    def conclude(first_q, q_blocks):
        column = lane_iota((1, SEG)).astype(jnp.float32)
        for q in range(first_q, first_q + q_blocks):

            def one_row(row, carry, q=q):
                t = acc[row, :, q * SEG : (q + 1) * SEG]
                inverse = 1.0 / t[C : C + 1]
                found[q, row] = (t[:C] * inverse).astype(jnp.bfloat16)
                hops = float(top + q) - t[C + 2 : C + 3] * inverse
                within = column - t[C + 1 : C + 2] * inverse
                disp[q, pl.ds(row, 1)] = hops + within * (1.0 / SEG)
                return carry

            lax.fori_loop(0, RG, one_row, 0, unroll=4)

            @pl.when(q != me)
            def _(q=q):
                for copy in give_back(q, me):
                    copy.start()

            @pl.when(q == me)
            def _(q=q):
                for copy in keep(q):
                    copy.start()

    attend(top, 4, 0, PLANE, 0, True)
    relay((4, 3))
    attend(top + 4, 4, 4, 4, 0, False)
    relay((2, 1, 0))
    attend(PLANE + 5, 4, 0, PLANE, 1, False)
    attend(PLANE + 1, 4, 0, PLANE, 1, False)
    for block in (7, 6, 5, 4):
        far(block).wait_recv()
        if block == 7:
            last.start()
    attend(5, 4, 0, PLANE, 2, False)
    conclude(5, 3)
    for block in (3, 2, 1, 0):
        far(block).wait_recv()
    attend(1, 4, 0, 5, 2, False)
    conclude(1, 4)
    last.wait()
    attend(0, 1, 0, 1, 3, False)
    conclude(0, 1)

    def sent(block, carry):
        near(block, keys.at[2 * PLANE + 1 + block]).wait_send()
        far(block).wait_send()
        return carry

    lax.fori_loop(0, PLANE, sent, 0)

    def returned(o, carry):
        for copy in give_back(block_of(o), block_of(o)):
            copy.wait_send()
            copy.wait_recv()
        return carry

    lax.fori_loop(1, PLANE, returned, 0)
    for copy in keep(me):
        copy.wait()


def features(ranges, images, w1, w2):
    anywhere = pl.BlockSpec(memory_space=pl.ANY)
    vmem = pl.BlockSpec(memory_space=pltpu.VMEM)
    dma = pltpu.SemaphoreType.DMA
    bf16 = jnp.bfloat16
    return pl.pallas_call(
        features_kernel,
        in_specs=[pl.BlockSpec(memory_space=pltpu.SMEM), anywhere, vmem, vmem],
        out_specs=(anywhere, anywhere),
        out_shape=(
            jax.ShapeDtypeStruct((PLANE, RG, C, SEG), bf16),
            jax.ShapeDtypeStruct((PLANE, RG, SEG), jnp.float32),
        ),
        scratch_shapes=[
            pltpu.VMEM((2, IMG_ROWS, C, SEG), bf16),
            pltpu.VMEM((2, EDGE_TILES, C, SEG), bf16),
            pltpu.VMEM((2, EDGE_TILES, C, SEG), bf16),
            pltpu.VMEM((2, EDGE_TILES, C, SEG), bf16),
            pltpu.VMEM((IMG_ROWS + EDGE_TILES, 3 * C, SEG), bf16),
            pltpu.VMEM((HID_ROWS + SLOT_ROWS, C, SEG), bf16),
            pltpu.VMEM((HID_ROWS, 3 * C, SEG), bf16),
            pltpu.VMEM((2, ROWS, C, SEG), bf16),
            pltpu.VMEM((2 * C, 12 * C), bf16),
            pltpu.VMEM((2 * C, 12 * C), bf16),
            pltpu.VMEM((PLANE, RG, C, SEG), bf16),
            pltpu.VMEM((KEYS + PLANE, RG, C, SEG), bf16),
            pltpu.VMEM((RG, VROWS, PLANE * SEG), jnp.float32),
            pltpu.VMEM((4 * SEG, PLANE * SEG), jnp.float32),
            pltpu.VMEM((PLANE, RG, C, SEG), bf16),
            pltpu.VMEM((PLANE, RG, SEG), jnp.float32),
            pltpu.VMEM((PLANE, 8, SEG), jnp.int32),
            pltpu.VMEM((PLANE, 8, SEG), jnp.int32),
            dma((2,)), dma((2, 2)), dma((2, 2)), dma((2, 2)), dma((2, 2)),
            dma((2, PLANE)), dma((2, PLANE)),
            dma((PLANE,)), dma((PLANE,)), dma((PLANE,)), dma((PLANE,)),
            dma, dma, dma((4,)),
            dma((PLANE,)), dma((PLANE,)), dma((PLANE,)), dma((PLANE,)), dma((PLANE,)), dma((PLANE,)),
        ],
        compiler_params=pltpu.CompilerParams(
            collective_id=0, has_side_effects=True, vmem_limit_bytes=48 * 1024 * 1024
        ),
        name="features",
    )(ranges, images, w1, w2)


def per_device(images, first_weight, second_weight, search_ranges):
    matched, disparity = features(
        search_ranges[:, :, 0], images.transpose(0, 2, 1, 3), first_weight, second_weight
    )
    return (
        matched.reshape(ROWS, C, SEG).transpose(1, 0, 2),
        disparity.reshape(ROWS, SEG),
    )


def solution(mesh):
    placed = (P(None, None, "rows", "cols"), P(), P(), P(None, "rows", "cols"))
    return jax.shard_map(
        per_device,
        mesh=mesh,
        in_specs=placed,
        out_specs=(P(None, "rows", "cols"), P("rows", "cols")),
        check_vma=False,
    )
```

```python
import functools

import jax
import jax.numpy as jnp
from jax import lax
from jax.experimental import pallas as pl
from jax.experimental.pallas import tpu as pltpu
from jax.sharding import PartitionSpec as P

C = 64
SEG = 128
RG = 8
D1 = 2
D2 = 4
EPS = 1e-05
SHARP = 10.0
LOG2E = 1.4426950408889634
ROWS = 64
HALO = D1 + D2
SLOTS = 8
SLOT_ROWS = (ROWS + 2 * D2) // SLOTS
EDGE_TILES = SLOT_ROWS + 2 * D1
IMG_ROWS = ROWS + 2 * HALO
HID_ROWS = ROWS + 2 * D2
PLANE = 8
KEYS = 2 * PLANE + 1
MESH = pl.DeviceIdType.MESH
VROWS = 80


def lane_iota(shape):
    return lax.broadcasted_iota(jnp.int32, shape, len(shape) - 1)


def roll(x, shift):
    return pltpu.roll(x, shift % SEG, x.ndim - 1)


def features_kernel(
    ranges, images, w1_ref, w2_ref, found_out, disp_out,
    img, edge, from_left, from_right, xs, hid, hs, unit, w1, w2,
    queries, keys, acc, bias, found, disp, range_tiles, range_all,
    load_sem, row_send, row_recv, col_send, col_recv,
    spread_send, spread_recv, near_send, near_recv, far_send, far_recv, last_send, last_recv, own_sem,
    range_send, range_recv, found_send, found_recv, disp_send, disp_recv,
):
    row_count, col_count = lax.axis_size("rows"), lax.axis_size("cols")
    x, col = lax.axis_index("rows"), lax.axis_index("cols")
    me = lax.rem(col, PLANE)
    base = col - me
    lane = lane_iota((C, SEG))

    def at_row(step):
        return (lax.rem(x + step + row_count, row_count), col)

    def at_col(step):
        return (x, lax.rem(col + step + col_count, col_count))

    barrier = pltpu.get_barrier_semaphore()
    friends = [at_row(1), at_row(-1), at_col(1), at_col(-1), at_col(PLANE), at_col(-PLANE)]
    friends += [(x, base + lax.rem(me + o, PLANE)) for o in range(1, PLANE)]
    for friend in friends:
        pl.semaphore_signal(barrier, inc=1, device_id=friend, device_id_type=MESH)

    loads = [
        pltpu.make_async_copy(images.at[n], img.at[n, pl.ds(HALO, ROWS)], load_sem.at[n])
        for n in range(2)
    ]
    loads[1].start()
    loads[0].start()
    pl.semaphore_wait(barrier, len(friends))

    def remote(src, dst, send, recv, device):
        return pltpu.make_async_remote_copy(
            src_ref=src, dst_ref=dst, send_sem=send, recv_sem=recv,
            device_id=device, device_id_type=MESH,
        )

    def row_copies(n):
        return (
            remote(
                images.at[n, pl.ds(ROWS - HALO, HALO)], img.at[n, pl.ds(0, HALO)],
                row_send.at[n, 0], row_recv.at[n, 0], at_row(1),
            ),
            remote(
                images.at[n, pl.ds(0, HALO)], img.at[n, pl.ds(HALO + ROWS, HALO)],
                row_send.at[n, 1], row_recv.at[n, 1], at_row(-1),
            ),
        )

    def col_copies(n):
        return (
            remote(edge.at[n], from_left.at[n], col_send.at[n, 0], col_recv.at[n, 0], at_col(1)),
            remote(edge.at[n], from_right.at[n], col_send.at[n, 1], col_recv.at[n, 1], at_col(-1)),
        )

    for copy in row_copies(1):
        copy.start()

    for group in range(PLANE):
        tile_row = lax.broadcasted_iota(jnp.int32, (8, SEG), 0)
        range_tiles[group] = jnp.where(tile_row == 0, ranges[0, group], ranges[1, group])

    def send_range(peer, slot):
        return remote(
            range_tiles.at[peer], range_all.at[slot],
            range_send.at[peer], range_recv.at[slot], (x, base + peer),
        )

    def start_range(o, carry):
        send_range(lax.rem(me + o, PLANE), me).start()
        return carry

    lax.fori_loop(1, PLANE, start_range, 0)
    range_all[me] = range_tiles[me]

    for ref, out in ((w1_ref, w1), (w2_ref, w2)):
        taps = jnp.concatenate([ref[t] for t in range(9)], axis=1)
        none = jnp.zeros((C, 3 * C), jnp.bfloat16)
        out[0:C] = jnp.concatenate([taps, none], axis=1)
        out[C:] = jnp.concatenate([none, taps], axis=1)

    def send_edges(n):
        loads[n].wait()
        for copy in row_copies(n):
            copy.wait()

        @pl.when(x == 0)
        def _():
            img[n, 0:HALO] = jnp.zeros((HALO, C, SEG), jnp.bfloat16)

        @pl.when(x == row_count - 1)
        def _():
            img[n, HALO + ROWS :] = jnp.zeros((HALO, C, SEG), jnp.bfloat16)

        def pack(tile, carry):
            packed = jnp.zeros((C, SEG), jnp.bfloat16)
            for slot in range(SLOTS):
                row = img[n, SLOT_ROWS * slot + tile]
                start = 16 * slot
                packed = jnp.where((lane >= start) & (lane < start + 8), roll(row, start + 6), packed)
                packed = jnp.where((lane >= start + 8) & (lane < start + 16), roll(row, start + 10), packed)
            edge[n, tile] = packed
            return carry

        lax.fori_loop(0, EDGE_TILES, pack, 0)
        for copy in col_copies(n):
            copy.start()

    send_edges(1)
    for copy in row_copies(0):
        copy.start()

    climbs = 1 - lax.rem(me, 2)

    def group_at(s):
        return lax.rem(me + 2 * PLANE + (2 * climbs - 1) * s, PLANE)

    part = lane % 16
    inner = (part >= 6) & (part < 10)
    low_part = part < 6
    left_open = jnp.where(col == 0, 0.0, 1.0)
    right_open = jnp.where(col == col_count - 1, 0.0, 1.0)
    open_side = jnp.where(part < 8, left_open, right_open)
    first_row = x * ROWS - D2
    height = row_count * ROWS
    slot_row = SLOT_ROWS * (lane // 16) + first_row

    def shifted(read, edges, rows, dest, dilation, first_left, first_right):
        for slot in range(SLOTS):
            low = slot * SLOT_ROWS
            high = rows if slot == SLOTS - 1 else low + SLOT_ROWS

            def one(row, carry, slot=slot, low=low):
                value = read(row)
                tile = edges(row - low)
                dest[row, 0:C] = jnp.where(
                    lane < dilation, roll(tile, -(16 * slot + first_left)), roll(value, dilation)
                )
                dest[row, C : 2 * C] = value
                dest[row, 2 * C :] = jnp.where(
                    lane >= SEG - dilation,
                    roll(tile, SEG - dilation - 16 * slot - first_right),
                    roll(value, -dilation),
                )
                return carry

            lax.fori_loop(low, high, one, 0, unroll=3)

    def window(ref, row, step, count):
        return jnp.concatenate([ref[row + step * t] for t in range(count)], axis=0)

    def pairs(weights, ref, rows, step):
        both = jnp.concatenate([window(ref, row, step, 4) for row in rows], axis=1)
        return jnp.dot(weights[...], both, preferred_element_type=jnp.float32)

    def silu(v):
        half = 0.5 * v
        return half + half * jnp.tanh(half)

    def spread(n, group):
        out = keys.at[2 * PLANE + 1 + me] if n else queries.at[me]
        return remote(
            unit.at[n, pl.ds(RG * group, RG)], out,
            spread_send.at[n, group], spread_recv.at[n, me], (x, base + group),
        )

    def arrived(n, source):
        out = keys.at[2 * PLANE + 1 + source] if n else queries.at[source]
        remote(
            unit.at[n, pl.ds(RG * source, RG)], out,
            spread_send.at[n, source], spread_recv.at[n, source], (x, base + source),
        ).wait_recv()

    def convolve(n, middle, each, shifts_done, after):
        for copy in col_copies(n):
            copy.wait()

        def merge(tile, carry):
            ours = edge[n, tile]
            left = from_left[n, tile] * left_open.astype(jnp.bfloat16)
            right = from_right[n, tile] * right_open.astype(jnp.bfloat16)
            value = jnp.where(inner, ours, jnp.where(low_part, left, right))
            edge[n, tile] = value
            dest = IMG_ROWS + tile
            xs[dest, 0:C] = roll(value, D1)
            xs[dest, C : 2 * C] = value
            xs[dest, 2 * C :] = roll(value, -D1)
            return carry

        lax.fori_loop(0, EDGE_TILES, merge, 0)
        shifted(lambda row: img[n, row], lambda t: edge[n, t], IMG_ROWS, xs, D1, 4, 10)
        shifts_done()
        def packed_hidden(tile, act):
            at = slot_row + tile
            inside = jnp.where((at >= 0) & (at < height), open_side, 0.0)
            hid[HID_ROWS + tile] = (act * inside).astype(jnp.bfloat16)

        def conv1_packed(step, carry):
            tile = 4 * step
            act = silu(pairs(w1, xs, (IMG_ROWS + tile, IMG_ROWS + tile + 1), D1))
            for a in range(2):
                for b in range(2):
                    value = act[C * a : C * (a + 1), SEG * b : SEG * (b + 1)]
                    packed_hidden(tile + 2 * a + b, value)
            return carry

        lax.fori_loop(0, SLOT_ROWS // 4, conv1_packed, 0, unroll=2)
        tile = SLOT_ROWS - 1
        end = window(xs, IMG_ROWS + tile, D1, 3)
        packed_hidden(tile, silu(jnp.dot(w1[0:C, 0 : 9 * C], end, preferred_element_type=jnp.float32)))

        def hidden_rows(block):
            row = RG * block
            starts = (row, row + 1, row + 4, row + 5)
            act = silu(pairs(w1, xs, starts, D1))
            for a in range(2):
                for b, start in enumerate(starts):
                    at = first_row + start + 2 * a
                    inside = jnp.where((at >= 0) & (at < height), 1.0, 0.0)
                    value = act[C * a : C * (a + 1), SEG * b : SEG * (b + 1)] * inside
                    value = value.astype(jnp.bfloat16)
                    hid[start + 2 * a] = value
            for step in range(RG):
                at = row + step
                slot = at // SLOT_ROWS
                value = hid[at]
                tile = hid[HID_ROWS + at - SLOT_ROWS * slot]
                from_low = pltpu.roll(tile, lax.rem(2 * SEG - 16 * slot - 2, SEG), 1)
                from_high = pltpu.roll(tile, lax.rem(2 * SEG - D2 - 16 * slot - 10, SEG), 1)
                hs[at, 0:C] = jnp.where(lane < D2, from_low, roll(value, D2))
                hs[at, C : 2 * C] = value
                hs[at, 2 * C :] = jnp.where(lane >= SEG - D2, from_high, roll(value, -D2))

        def unit_rows(group):
            row = RG * group
            total = pairs(w2, hs, (row, row + 1, row + 2, row + 3), D2)
            for a in range(2):
                for b in range(4):
                    at = row + 4 * a + b
                    value = total[C * a : C * (a + 1), SEG * b : SEG * (b + 1)]
                    feats = (img[n, HALO + at].astype(jnp.float32) + value).astype(jnp.bfloat16)
                    feats = feats.astype(jnp.float32)
                    scale = lax.rsqrt(jnp.mean(feats * feats, axis=0, keepdims=True) + EPS)
                    unit[n, at] = (feats * scale).astype(jnp.bfloat16)

        def step(s, carry, act=None):
            group = group_at(s)
            unit_rows(group)
            following = group_at(s + 1)
            hidden_rows(following + climbs)

            @pl.when(following == (PLANE - 1) * (1 - climbs))
            def _():
                hidden_rows(PLANE * (1 - climbs))

            @pl.when(s > 0)
            def _():
                spread(n, group).start()

            if act is not None:
                act(s)
            return carry

        hidden_rows(me)
        hidden_rows(me + 1)
        step(0, 0)
        after(0)
        lax.fori_loop(1, 3, step, 0)
        middle()
        lax.fori_loop(3, PLANE - 1, functools.partial(step, act=each), 0)
        group = group_at(PLANE - 1)
        unit_rows(group)
        spread(n, group).start()
        after(1)

    def near(block, src):
        return remote(
            src, keys.at[PLANE + 1 + block], near_send.at[block], near_recv.at[block], at_col(PLANE)
        )

    def far(block):
        return remote(
            keys.at[PLANE + 1 + block], keys.at[1 + block],
            far_send.at[block], far_recv.at[block], at_col(PLANE),
        )

    last = remote(keys.at[PLANE], keys.at[0], last_send, last_recv, at_col(PLANE))
    own_k = pltpu.make_async_copy(
        unit.at[1, pl.ds(RG * me, RG)], keys.at[2 * PLANE + 1 + me], own_sem.at[1]
    )

    def block_of(o):
        return lax.rem(me + o, PLANE)

    def forward(age):
        block = lax.rem(me + PLANE + (2 * lax.rem(me + age, 2) - 1) * age, PLANE)
        arrived(1, block)
        near(block, keys.at[2 * PLANE + 1 + block]).start()

    def right_each(s):
        @pl.when(s == PLANE - 2)
        def _():
            forward(1)

    def right_after(stage):
        if stage == 0:
            own_k.start()
            near(me, unit.at[1, pl.ds(RG * me, RG)]).start()

    def left_shifts():
        forward(2)
        forward(3)

    def left_after(stage):
        if stage == 0:
            forward(4)
            forward(5)
        else:
            forward(7)


    def relay(blocks):
        for block in blocks:
            near(block, keys.at[2 * PLANE + 1 + block]).wait_recv()
            far(block).start()

    convolve(1, lambda: send_edges(0), right_each, lambda: None, right_after)
    convolve(0, lambda: forward(6), None, left_shifts, left_after)
    own_q = pltpu.make_async_copy(unit.at[0, pl.ds(RG * me, RG)], queries.at[me], own_sem.at[0])
    own_q.start()

    def finish_spread(o, carry):
        block = block_of(o)
        arrived(0, block)
        send_range(block, block).wait_recv()
        send_range(block, block).wait_send()
        for n in range(2):
            spread(n, block).wait_send()
        return carry

    lax.fori_loop(1, PLANE, finish_spread, 0)
    own_k.wait()
    own_q.wait()

    scale = SHARP / C * LOG2E
    plane = col // PLANE
    top = 2 * PLANE + 1

    def attend(first_key, key_blocks, first_q, q_blocks, needed, fresh, unroll):
        width, depth = q_blocks * SEG, key_blocks * SEG
        span = pl.ds(first_q * SEG, width)
        within = lane_iota((1, SEG))
        upper = jnp.concatenate(
            [SEG * (top + q - range_all[q, 0:1]) + within for q in range(first_q, first_q + q_blocks)],
            axis=1,
        )
        lower = jnp.concatenate(
            [
                SEG * (top + q - range_all[q, 0:1] - range_all[q, 1:2]) + within
                for q in range(first_q, first_q + q_blocks)
            ],
            axis=1,
        )

        def mask(step, carry):
            at = 64 * step
            key = SEG * first_key + at + lax.broadcasted_iota(jnp.int32, (64, width), 0)
            inside = (key <= upper) & (key > lower)
            bias[pl.ds(pl.multiple_of(at, 64), 64), 0:width] = jnp.where(inside, 0.0, -1e30)
            return carry

        lax.fori_loop(0, depth // 64, mask, 0)
        present = jnp.where(plane >= needed, 1.0, 0.0).astype(jnp.bfloat16)
        near_present = jnp.where(plane >= 2, 1.0, 0.0).astype(jnp.bfloat16)
        extra_row = lax.broadcasted_iota(jnp.int32, (16, SEG), 0)
        column = lane_iota((16, SEG)).astype(jnp.float32)
        extra = jnp.concatenate(
            [
                jnp.where(
                    extra_row == 0,
                    1.0,
                    jnp.where(extra_row == 1, column, jnp.where(extra_row == 2, float(first_key + b), 0.0)),
                )
                for b in range(key_blocks)
            ],
            axis=1,
        ).astype(jnp.bfloat16)

        def one_row(row, carry):
            chunk = jnp.concatenate([keys[first_key + b, row] for b in range(key_blocks)], axis=1)
            if needed == 3:
                chunk = jnp.concatenate([chunk[:, :SEG] * present, chunk[:, SEG:] * near_present], axis=1)
            elif needed:
                chunk = chunk * present
            q = jnp.concatenate([queries[first_q + b, row] for b in range(q_blocks)], axis=1)
            s = jnp.dot(chunk.T, q, preferred_element_type=jnp.float32)
            p = jnp.exp2(s * scale + bias[0:depth, 0:width]).astype(jnp.bfloat16)
            values = jnp.concatenate([chunk, extra], axis=0)
            total = jnp.dot(values, p, preferred_element_type=jnp.float32)
            if fresh:
                acc[row, :, span] = total
            else:
                acc[row, :, span] += total
            return carry

        lax.fori_loop(0, RG, one_row, 0, unroll=unroll)

    def give_back(peer, slot):
        return [
            remote(
                found.at[peer], found_out.at[slot],
                found_send.at[peer], found_recv.at[slot], (x, base + peer),
            ),
            remote(
                disp.at[peer], disp_out.at[slot],
                disp_send.at[peer], disp_recv.at[slot], (x, base + peer),
            ),
        ]

    def keep(slot):
        return [
            pltpu.make_async_copy(found.at[slot], found_out.at[slot], own_sem.at[2]),
            pltpu.make_async_copy(disp.at[slot], disp_out.at[slot], own_sem.at[3]),
        ]

    def conclude(first_q, q_blocks):
        column = lane_iota((1, SEG)).astype(jnp.float32)
        for q in range(first_q, first_q + q_blocks):

            def one_row(row, carry, q=q):
                t = acc[row, :, q * SEG : (q + 1) * SEG]
                inverse = 1.0 / t[C : C + 1]
                found[q, row] = (t[:C] * inverse).astype(jnp.bfloat16)
                hops = float(top + q) - t[C + 2 : C + 3] * inverse
                within = column - t[C + 1 : C + 2] * inverse
                disp[q, pl.ds(row, 1)] = hops + within * (1.0 / SEG)
                return carry

            lax.fori_loop(0, RG, one_row, 0, unroll=4)

            @pl.when(q != me)
            def _(q=q):
                for copy in give_back(q, me):
                    copy.start()

            @pl.when(q == me)
            def _(q=q):
                for copy in keep(q):
                    copy.start()

    relay((7, 6, 5))
    attend(top, 4, 0, PLANE, 0, True, 4)
    relay((4, 3))
    attend(top + 4, 4, 4, 4, 0, False, 8)
    relay((2,))
    attend(PLANE + 5, 4, 0, PLANE, 1, False, 4)
    relay((1, 0))
    far(7).wait_recv()
    last.start()
    attend(PLANE + 1, 4, 0, PLANE, 1, False, 4)
    far(6).wait_recv()
    far(5).wait_recv()
    attend(6, 3, 0, 8, 2, False, 4)
    conclude(6, 2)
    far(4).wait_recv()
    far(3).wait_recv()
    attend(4, 2, 0, 6, 2, False, 8)
    conclude(4, 2)
    far(2).wait_recv()
    far(1).wait_recv()
    attend(2, 2, 0, 4, 2, False, 8)
    conclude(2, 2)
    far(0).wait_recv()
    last.wait()
    attend(0, 2, 0, 2, 3, False, 8)
    conclude(0, 2)

    def sent(block, carry):
        near(block, keys.at[2 * PLANE + 1 + block]).wait_send()
        far(block).wait_send()
        return carry

    lax.fori_loop(0, PLANE, sent, 0)

    def returned(o, carry):
        for copy in give_back(block_of(o), block_of(o)):
            copy.wait_send()
            copy.wait_recv()
        return carry

    lax.fori_loop(1, PLANE, returned, 0)
    for copy in keep(me):
        copy.wait()


def features(ranges, images, w1, w2):
    anywhere = pl.BlockSpec(memory_space=pl.ANY)
    vmem = pl.BlockSpec(memory_space=pltpu.VMEM)
    dma = pltpu.SemaphoreType.DMA
    bf16 = jnp.bfloat16
    return pl.pallas_call(
        features_kernel,
        in_specs=[pl.BlockSpec(memory_space=pltpu.SMEM), anywhere, vmem, vmem],
        out_specs=(anywhere, anywhere),
        out_shape=(
            jax.ShapeDtypeStruct((PLANE, RG, C, SEG), bf16),
            jax.ShapeDtypeStruct((PLANE, RG, SEG), jnp.float32),
        ),
        scratch_shapes=[
            pltpu.VMEM((2, IMG_ROWS, C, SEG), bf16),
            pltpu.VMEM((2, EDGE_TILES, C, SEG), bf16),
            pltpu.VMEM((2, EDGE_TILES, C, SEG), bf16),
            pltpu.VMEM((2, EDGE_TILES, C, SEG), bf16),
            pltpu.VMEM((IMG_ROWS + EDGE_TILES, 3 * C, SEG), bf16),
            pltpu.VMEM((HID_ROWS + SLOT_ROWS, C, SEG), bf16),
            pltpu.VMEM((HID_ROWS, 3 * C, SEG), bf16),
            pltpu.VMEM((2, ROWS, C, SEG), bf16),
            pltpu.VMEM((2 * C, 12 * C), bf16),
            pltpu.VMEM((2 * C, 12 * C), bf16),
            pltpu.VMEM((PLANE, RG, C, SEG), bf16),
            pltpu.VMEM((KEYS + PLANE, RG, C, SEG), bf16),
            pltpu.VMEM((RG, VROWS, PLANE * SEG), jnp.float32),
            pltpu.VMEM((4 * SEG, PLANE * SEG), jnp.float32),
            pltpu.VMEM((PLANE, RG, C, SEG), bf16),
            pltpu.VMEM((PLANE, RG, SEG), jnp.float32),
            pltpu.VMEM((PLANE, 8, SEG), jnp.int32),
            pltpu.VMEM((PLANE, 8, SEG), jnp.int32),
            dma((2,)), dma((2, 2)), dma((2, 2)), dma((2, 2)), dma((2, 2)),
            dma((2, PLANE)), dma((2, PLANE)),
            dma((PLANE,)), dma((PLANE,)), dma((PLANE,)), dma((PLANE,)),
            dma, dma, dma((4,)),
            dma((PLANE,)), dma((PLANE,)), dma((PLANE,)), dma((PLANE,)), dma((PLANE,)), dma((PLANE,)),
        ],
        compiler_params=pltpu.CompilerParams(
            collective_id=0, has_side_effects=True, vmem_limit_bytes=48 * 1024 * 1024
        ),
        name="features",
    )(ranges, images, w1, w2)


def per_device(images, first_weight, second_weight, search_ranges):
    matched, disparity = features(
        search_ranges[:, :, 0], images.transpose(0, 2, 1, 3), first_weight, second_weight
    )
    return (
        matched.reshape(ROWS, C, SEG).transpose(1, 0, 2),
        disparity.reshape(ROWS, SEG),
    )


def solution(mesh):
    placed = (P(None, None, "rows", "cols"), P(), P(), P(None, "rows", "cols"))
    return jax.shard_map(
        per_device,
        mesh=mesh,
        in_specs=placed,
        out_specs=(P(None, "rows", "cols"), P("rows", "cols")),
        check_vma=False,
    )
```

```python
import functools

import jax
import jax.numpy as jnp
from jax import lax
from jax.experimental import pallas as pl
from jax.experimental.pallas import tpu as pltpu
from jax.sharding import PartitionSpec as P

C = 64
SEG = 128
RG = 8
D1 = 2
D2 = 4
EPS = 1e-05
SHARP = 10.0
LOG2E = 1.4426950408889634
ROWS = 64
HALO = D1 + D2
SLOTS = 8
SLOT_ROWS = (ROWS + 2 * D2) // SLOTS
EDGE_TILES = SLOT_ROWS + 2 * D1
IMG_ROWS = ROWS + 2 * HALO
HID_ROWS = ROWS + 2 * D2
PLANE = 8
KEYS = 2 * PLANE + 1
MESH = pl.DeviceIdType.MESH
VROWS = 80


def lane_iota(shape):
    return lax.broadcasted_iota(jnp.int32, shape, len(shape) - 1)


def roll(x, shift):
    return pltpu.roll(x, shift % SEG, x.ndim - 1)


def features_kernel(
    ranges, images, w1_ref, w2_ref, found_out, disp_out,
    img, edge, from_left, from_right, xs, hid, hs, unit, w1, w2,
    queries, keys, acc, bias, found, disp, range_tiles, range_all,
    load_sem, row_send, row_recv, col_send, col_recv,
    spread_send, spread_recv, near_send, near_recv, far_send, far_recv, last_send, last_recv, own_sem,
    range_send, range_recv, found_send, found_recv, disp_send, disp_recv,
):
    row_count, col_count = lax.axis_size("rows"), lax.axis_size("cols")
    x, col = lax.axis_index("rows"), lax.axis_index("cols")
    me = lax.rem(col, PLANE)
    base = col - me
    lane = lane_iota((C, SEG))

    def at_row(step):
        return (lax.rem(x + step + row_count, row_count), col)

    def at_col(step):
        return (x, lax.rem(col + step + col_count, col_count))

    barrier = pltpu.get_barrier_semaphore()
    friends = [at_row(1), at_row(-1), at_col(1), at_col(-1), at_col(PLANE), at_col(-PLANE)]
    friends += [(x, base + lax.rem(me + o, PLANE)) for o in range(1, PLANE)]
    for friend in friends:
        pl.semaphore_signal(barrier, inc=1, device_id=friend, device_id_type=MESH)

    loads = [
        pltpu.make_async_copy(images.at[n], img.at[n, pl.ds(HALO, ROWS)], load_sem.at[n])
        for n in range(2)
    ]
    loads[1].start()
    loads[0].start()
    pl.semaphore_wait(barrier, len(friends))

    def remote(src, dst, send, recv, device):
        return pltpu.make_async_remote_copy(
            src_ref=src, dst_ref=dst, send_sem=send, recv_sem=recv,
            device_id=device, device_id_type=MESH,
        )

    def row_copies(n):
        return (
            remote(
                images.at[n, pl.ds(ROWS - HALO, HALO)], img.at[n, pl.ds(0, HALO)],
                row_send.at[n, 0], row_recv.at[n, 0], at_row(1),
            ),
            remote(
                images.at[n, pl.ds(0, HALO)], img.at[n, pl.ds(HALO + ROWS, HALO)],
                row_send.at[n, 1], row_recv.at[n, 1], at_row(-1),
            ),
        )

    def col_copies(n):
        return (
            remote(edge.at[n], from_left.at[n], col_send.at[n, 0], col_recv.at[n, 0], at_col(1)),
            remote(edge.at[n], from_right.at[n], col_send.at[n, 1], col_recv.at[n, 1], at_col(-1)),
        )

    for copy in row_copies(1):
        copy.start()

    for group in range(PLANE):
        tile_row = lax.broadcasted_iota(jnp.int32, (8, SEG), 0)
        range_tiles[group] = jnp.where(tile_row == 0, ranges[0, group], ranges[1, group])

    def send_range(peer, slot):
        return remote(
            range_tiles.at[peer], range_all.at[slot],
            range_send.at[peer], range_recv.at[slot], (x, base + peer),
        )

    def start_range(o, carry):
        send_range(lax.rem(me + o, PLANE), me).start()
        return carry

    lax.fori_loop(1, PLANE, start_range, 0)
    range_all[me] = range_tiles[me]

    for ref, out in ((w1_ref, w1), (w2_ref, w2)):
        taps = jnp.concatenate([ref[t] for t in range(9)], axis=1)
        none = jnp.zeros((C, 3 * C), jnp.bfloat16)
        out[0:C] = jnp.concatenate([taps, none], axis=1)
        out[C:] = jnp.concatenate([none, taps], axis=1)

    def send_edges(n):
        loads[n].wait()
        for copy in row_copies(n):
            copy.wait()

        @pl.when(x == 0)
        def _():
            img[n, 0:HALO] = jnp.zeros((HALO, C, SEG), jnp.bfloat16)

        @pl.when(x == row_count - 1)
        def _():
            img[n, HALO + ROWS :] = jnp.zeros((HALO, C, SEG), jnp.bfloat16)

        def pack(tile, carry):
            packed = jnp.zeros((C, SEG), jnp.bfloat16)
            for slot in range(SLOTS):
                row = img[n, SLOT_ROWS * slot + tile]
                start = 16 * slot
                packed = jnp.where((lane >= start) & (lane < start + 8), roll(row, start + 6), packed)
                packed = jnp.where((lane >= start + 8) & (lane < start + 16), roll(row, start + 10), packed)
            edge[n, tile] = packed
            return carry

        lax.fori_loop(0, EDGE_TILES, pack, 0)
        for copy in col_copies(n):
            copy.start()

    send_edges(1)
    for copy in row_copies(0):
        copy.start()

    climbs = 1 - lax.rem(me, 2)

    def group_at(s):
        return lax.rem(me + 2 * PLANE + (2 * climbs - 1) * s, PLANE)

    part = lane % 16
    inner = (part >= 6) & (part < 10)
    low_part = part < 6
    left_open = jnp.where(col == 0, 0.0, 1.0)
    right_open = jnp.where(col == col_count - 1, 0.0, 1.0)
    open_side = jnp.where(part < 8, left_open, right_open)
    first_row = x * ROWS - D2
    height = row_count * ROWS
    slot_row = SLOT_ROWS * (lane // 16) + first_row

    def shifted(read, edges, rows, dest, dilation, first_left, first_right):
        for slot in range(SLOTS):
            low = slot * SLOT_ROWS
            high = rows if slot == SLOTS - 1 else low + SLOT_ROWS

            def one(row, carry, slot=slot, low=low):
                value = read(row)
                tile = edges(row - low)
                dest[row, 0:C] = jnp.where(
                    lane < dilation, roll(tile, -(16 * slot + first_left)), roll(value, dilation)
                )
                dest[row, C : 2 * C] = value
                dest[row, 2 * C :] = jnp.where(
                    lane >= SEG - dilation,
                    roll(tile, SEG - dilation - 16 * slot - first_right),
                    roll(value, -dilation),
                )
                return carry

            lax.fori_loop(low, high, one, 0, unroll=3)

    def window(ref, row, step, count):
        return jnp.concatenate([ref[row + step * t] for t in range(count)], axis=0)

    def pairs(weights, ref, rows, step):
        both = jnp.concatenate([window(ref, row, step, 4) for row in rows], axis=1)
        return jnp.dot(weights[...], both, preferred_element_type=jnp.float32)

    def silu(v):
        half = 0.5 * v
        return half + half * jnp.tanh(half)

    def spread(n, group):
        out = keys.at[2 * PLANE + 1 + me] if n else queries.at[me]
        return remote(
            unit.at[n, pl.ds(RG * group, RG)], out,
            spread_send.at[n, group], spread_recv.at[n, me], (x, base + group),
        )

    def arrived(n, source):
        out = keys.at[2 * PLANE + 1 + source] if n else queries.at[source]
        remote(
            unit.at[n, pl.ds(RG * source, RG)], out,
            spread_send.at[n, source], spread_recv.at[n, source], (x, base + source),
        ).wait_recv()

    def convolve(n, middle, each, shifts_done, after):
        for copy in col_copies(n):
            copy.wait()

        def merge(tile, carry):
            ours = edge[n, tile]
            left = from_left[n, tile] * left_open.astype(jnp.bfloat16)
            right = from_right[n, tile] * right_open.astype(jnp.bfloat16)
            value = jnp.where(inner, ours, jnp.where(low_part, left, right))
            edge[n, tile] = value
            dest = IMG_ROWS + tile
            xs[dest, 0:C] = roll(value, D1)
            xs[dest, C : 2 * C] = value
            xs[dest, 2 * C :] = roll(value, -D1)
            return carry

        lax.fori_loop(0, EDGE_TILES, merge, 0)
        shifted(lambda row: img[n, row], lambda t: edge[n, t], IMG_ROWS, xs, D1, 4, 10)
        shifts_done()
        def packed_hidden(tile, act):
            at = slot_row + tile
            inside = jnp.where((at >= 0) & (at < height), open_side, 0.0)
            hid[HID_ROWS + tile] = (act * inside).astype(jnp.bfloat16)

        def conv1_packed(step, carry):
            tile = 4 * step
            act = silu(pairs(w1, xs, (IMG_ROWS + tile, IMG_ROWS + tile + 1), D1))
            for a in range(2):
                for b in range(2):
                    value = act[C * a : C * (a + 1), SEG * b : SEG * (b + 1)]
                    packed_hidden(tile + 2 * a + b, value)
            return carry

        lax.fori_loop(0, SLOT_ROWS // 4, conv1_packed, 0, unroll=2)
        tile = SLOT_ROWS - 1
        end = window(xs, IMG_ROWS + tile, D1, 3)
        packed_hidden(tile, silu(jnp.dot(w1[0:C, 0 : 9 * C], end, preferred_element_type=jnp.float32)))

        def hidden_rows(block):
            row = RG * block
            starts = (row, row + 1, row + 4, row + 5)
            act = silu(pairs(w1, xs, starts, D1))
            for a in range(2):
                for b, start in enumerate(starts):
                    at = first_row + start + 2 * a
                    inside = jnp.where((at >= 0) & (at < height), 1.0, 0.0)
                    value = act[C * a : C * (a + 1), SEG * b : SEG * (b + 1)] * inside
                    value = value.astype(jnp.bfloat16)
                    hid[start + 2 * a] = value
            for step in range(RG):
                at = row + step
                slot = at // SLOT_ROWS
                value = hid[at]
                tile = hid[HID_ROWS + at - SLOT_ROWS * slot]
                from_low = pltpu.roll(tile, lax.rem(2 * SEG - 16 * slot - 2, SEG), 1)
                from_high = pltpu.roll(tile, lax.rem(2 * SEG - D2 - 16 * slot - 10, SEG), 1)
                hs[at, 0:C] = jnp.where(lane < D2, from_low, roll(value, D2))
                hs[at, C : 2 * C] = value
                hs[at, 2 * C :] = jnp.where(lane >= SEG - D2, from_high, roll(value, -D2))

        def unit_rows(group):
            row = RG * group
            total = pairs(w2, hs, (row, row + 1, row + 2, row + 3), D2)
            for a in range(2):
                for b in range(4):
                    at = row + 4 * a + b
                    value = total[C * a : C * (a + 1), SEG * b : SEG * (b + 1)]
                    feats = (img[n, HALO + at].astype(jnp.float32) + value).astype(jnp.bfloat16)
                    feats = feats.astype(jnp.float32)
                    scale = lax.rsqrt(jnp.mean(feats * feats, axis=0, keepdims=True) + EPS)
                    unit[n, at] = (feats * scale).astype(jnp.bfloat16)

        def step(s, carry, act=None):
            group = group_at(s)
            unit_rows(group)
            following = group_at(s + 1)
            hidden_rows(following + climbs)

            @pl.when(following == (PLANE - 1) * (1 - climbs))
            def _():
                hidden_rows(PLANE * (1 - climbs))

            @pl.when(s > 0)
            def _():
                spread(n, group).start()

            if act is not None:
                act(s)
            return carry

        hidden_rows(me)
        hidden_rows(me + 1)
        step(0, 0)
        after(0)
        lax.fori_loop(1, 3, step, 0)
        middle()
        lax.fori_loop(3, PLANE - 1, functools.partial(step, act=each), 0)
        group = group_at(PLANE - 1)
        unit_rows(group)
        spread(n, group).start()
        after(1)

    def near(block, src):
        return remote(
            src, keys.at[PLANE + 1 + block], near_send.at[block], near_recv.at[block], at_col(PLANE)
        )

    def far(block):
        return remote(
            keys.at[PLANE + 1 + block], keys.at[1 + block],
            far_send.at[block], far_recv.at[block], at_col(PLANE),
        )

    last = remote(keys.at[PLANE], keys.at[0], last_send, last_recv, at_col(PLANE))
    own_k = pltpu.make_async_copy(
        unit.at[1, pl.ds(RG * me, RG)], keys.at[2 * PLANE + 1 + me], own_sem.at[1]
    )

    def block_of(o):
        return lax.rem(me + o, PLANE)

    def forward(age):
        block = lax.rem(me + PLANE + (2 * lax.rem(me + age, 2) - 1) * age, PLANE)
        arrived(1, block)
        near(block, keys.at[2 * PLANE + 1 + block]).start()

    def right_each(s):
        @pl.when(s == PLANE - 2)
        def _():
            forward(1)

    def right_after(stage):
        if stage == 0:
            own_k.start()
            near(me, unit.at[1, pl.ds(RG * me, RG)]).start()

    def left_shifts():
        forward(2)
        forward(3)

    def left_after(stage):
        if stage == 0:
            forward(4)
            forward(5)
        else:
            forward(7)


    def relay(blocks):
        for block in blocks:
            near(block, keys.at[2 * PLANE + 1 + block]).wait_recv()
            far(block).start()

    convolve(1, lambda: send_edges(0), right_each, lambda: None, right_after)
    convolve(0, lambda: forward(6), None, left_shifts, left_after)
    relay((7, 6, 5, 4))
    own_q = pltpu.make_async_copy(unit.at[0, pl.ds(RG * me, RG)], queries.at[me], own_sem.at[0])
    own_q.start()

    def finish_spread(o, carry):
        block = block_of(o)
        arrived(0, block)
        send_range(block, block).wait_recv()
        send_range(block, block).wait_send()
        for n in range(2):
            spread(n, block).wait_send()
        return carry

    lax.fori_loop(1, PLANE, finish_spread, 0)
    own_k.wait()
    own_q.wait()

    scale = SHARP / C * LOG2E
    plane = col // PLANE
    top = 2 * PLANE + 1

    def attend(first_key, key_blocks, first_q, q_blocks, needed, fresh, unroll):
        width, depth = q_blocks * SEG, key_blocks * SEG
        span = pl.ds(first_q * SEG, width)
        within = lane_iota((1, SEG))
        upper = jnp.concatenate(
            [SEG * (top + q - range_all[q, 0:1]) + within for q in range(first_q, first_q + q_blocks)],
            axis=1,
        )
        lower = jnp.concatenate(
            [
                SEG * (top + q - range_all[q, 0:1] - range_all[q, 1:2]) + within
                for q in range(first_q, first_q + q_blocks)
            ],
            axis=1,
        )

        def mask(step, carry):
            at = 64 * step
            key = SEG * first_key + at + lax.broadcasted_iota(jnp.int32, (64, width), 0)
            inside = (key <= upper) & (key > lower)
            bias[pl.ds(pl.multiple_of(at, 64), 64), 0:width] = jnp.where(inside, 0.0, -1e30)
            return carry

        lax.fori_loop(0, depth // 64, mask, 0)
        present = jnp.where(plane >= needed, 1.0, 0.0).astype(jnp.bfloat16)
        extra_row = lax.broadcasted_iota(jnp.int32, (16, SEG), 0)
        column = lane_iota((16, SEG)).astype(jnp.float32)
        extra = jnp.concatenate(
            [
                jnp.where(
                    extra_row == 0,
                    1.0,
                    jnp.where(extra_row == 1, column, jnp.where(extra_row == 2, float(first_key + b), 0.0)),
                )
                for b in range(key_blocks)
            ],
            axis=1,
        ).astype(jnp.bfloat16)

        def one_row(row, carry):
            chunk = jnp.concatenate([keys[first_key + b, row] for b in range(key_blocks)], axis=1)
            if needed:
                chunk = chunk * present
            q = jnp.concatenate([queries[first_q + b, row] for b in range(q_blocks)], axis=1)
            s = jnp.dot(chunk.T, q, preferred_element_type=jnp.float32)
            p = jnp.exp2(s * scale + bias[0:depth, 0:width]).astype(jnp.bfloat16)
            values = jnp.concatenate([chunk, extra], axis=0)
            total = jnp.dot(values, p, preferred_element_type=jnp.float32)
            if fresh:
                acc[row, :, span] = total
            else:
                acc[row, :, span] += total
            return carry

        lax.fori_loop(0, RG, one_row, 0, unroll=unroll)

    def give_back(peer, slot):
        return [
            remote(
                found.at[peer], found_out.at[slot],
                found_send.at[peer], found_recv.at[slot], (x, base + peer),
            ),
            remote(
                disp.at[peer], disp_out.at[slot],
                disp_send.at[peer], disp_recv.at[slot], (x, base + peer),
            ),
        ]

    def keep(slot):
        return [
            pltpu.make_async_copy(found.at[slot], found_out.at[slot], own_sem.at[2]),
            pltpu.make_async_copy(disp.at[slot], disp_out.at[slot], own_sem.at[3]),
        ]

    def conclude(first_q, q_blocks):
        column = lane_iota((1, SEG)).astype(jnp.float32)
        for q in range(first_q, first_q + q_blocks):

            def one_row(row, carry, q=q):
                t = acc[row, :, q * SEG : (q + 1) * SEG]
                inverse = 1.0 / t[C : C + 1]
                found[q, row] = (t[:C] * inverse).astype(jnp.bfloat16)
                hops = float(top + q) - t[C + 2 : C + 3] * inverse
                within = column - t[C + 1 : C + 2] * inverse
                disp[q, pl.ds(row, 1)] = hops + within * (1.0 / SEG)
                return carry

            lax.fori_loop(0, RG, one_row, 0, unroll=4)

            @pl.when(q != me)
            def _(q=q):
                for copy in give_back(q, me):
                    copy.start()

            @pl.when(q == me)
            def _(q=q):
                for copy in keep(q):
                    copy.start()

    attend(top, 4, 0, PLANE, 0, True, 4)
    relay((3, 2))
    far(7).wait_recv()
    last.start()
    attend(top + 4, 4, 4, 4, 0, False, 8)
    relay((1, 0))
    attend(PLANE + 5, 4, 0, PLANE, 1, False, 4)
    attend(PLANE + 1, 4, 0, PLANE, 1, False, 4)
    far(6).wait_recv()
    far(5).wait_recv()
    attend(6, 3, 0, 8, 2, False, 4)
    conclude(6, 2)
    far(4).wait_recv()
    far(3).wait_recv()
    attend(4, 2, 0, 6, 2, False, 8)
    conclude(4, 2)
    far(2).wait_recv()
    far(1).wait_recv()
    far(0).wait_recv()
    attend(1, 3, 0, 4, 2, False, 8)
    conclude(1, 3)
    last.wait()
    attend(0, 1, 0, 1, 3, False, 8)
    conclude(0, 1)

    def sent(block, carry):
        near(block, keys.at[2 * PLANE + 1 + block]).wait_send()
        far(block).wait_send()
        return carry

    lax.fori_loop(0, PLANE, sent, 0)

    def returned(o, carry):
        for copy in give_back(block_of(o), block_of(o)):
            copy.wait_send()
            copy.wait_recv()
        return carry

    lax.fori_loop(1, PLANE, returned, 0)
    for copy in keep(me):
        copy.wait()


def features(ranges, images, w1, w2):
    anywhere = pl.BlockSpec(memory_space=pl.ANY)
    vmem = pl.BlockSpec(memory_space=pltpu.VMEM)
    dma = pltpu.SemaphoreType.DMA
    bf16 = jnp.bfloat16
    return pl.pallas_call(
        features_kernel,
        in_specs=[pl.BlockSpec(memory_space=pltpu.SMEM), anywhere, vmem, vmem],
        out_specs=(anywhere, anywhere),
        out_shape=(
            jax.ShapeDtypeStruct((PLANE, RG, C, SEG), bf16),
            jax.ShapeDtypeStruct((PLANE, RG, SEG), jnp.float32),
        ),
        scratch_shapes=[
            pltpu.VMEM((2, IMG_ROWS, C, SEG), bf16),
            pltpu.VMEM((2, EDGE_TILES, C, SEG), bf16),
            pltpu.VMEM((2, EDGE_TILES, C, SEG), bf16),
            pltpu.VMEM((2, EDGE_TILES, C, SEG), bf16),
            pltpu.VMEM((IMG_ROWS + EDGE_TILES, 3 * C, SEG), bf16),
            pltpu.VMEM((HID_ROWS + SLOT_ROWS, C, SEG), bf16),
            pltpu.VMEM((HID_ROWS, 3 * C, SEG), bf16),
            pltpu.VMEM((2, ROWS, C, SEG), bf16),
            pltpu.VMEM((2 * C, 12 * C), bf16),
            pltpu.VMEM((2 * C, 12 * C), bf16),
            pltpu.VMEM((PLANE, RG, C, SEG), bf16),
            pltpu.VMEM((KEYS + PLANE, RG, C, SEG), bf16),
            pltpu.VMEM((RG, VROWS, PLANE * SEG), jnp.float32),
            pltpu.VMEM((4 * SEG, PLANE * SEG), jnp.float32),
            pltpu.VMEM((PLANE, RG, C, SEG), bf16),
            pltpu.VMEM((PLANE, RG, SEG), jnp.float32),
            pltpu.VMEM((PLANE, 8, SEG), jnp.int32),
            pltpu.VMEM((PLANE, 8, SEG), jnp.int32),
            dma((2,)), dma((2, 2)), dma((2, 2)), dma((2, 2)), dma((2, 2)),
            dma((2, PLANE)), dma((2, PLANE)),
            dma((PLANE,)), dma((PLANE,)), dma((PLANE,)), dma((PLANE,)),
            dma, dma, dma((4,)),
            dma((PLANE,)), dma((PLANE,)), dma((PLANE,)), dma((PLANE,)), dma((PLANE,)), dma((PLANE,)),
        ],
        compiler_params=pltpu.CompilerParams(
            collective_id=0, has_side_effects=True, vmem_limit_bytes=48 * 1024 * 1024
        ),
        name="features",
    )(ranges, images, w1, w2)


def per_device(images, first_weight, second_weight, search_ranges):
    matched, disparity = features(
        search_ranges[:, :, 0], images.transpose(0, 2, 1, 3), first_weight, second_weight
    )
    return (
        matched.reshape(ROWS, C, SEG).transpose(1, 0, 2),
        disparity.reshape(ROWS, SEG),
    )


def solution(mesh):
    placed = (P(None, None, "rows", "cols"), P(), P(), P(None, "rows", "cols"))
    return jax.shard_map(
        per_device,
        mesh=mesh,
        in_specs=placed,
        out_specs=(P(None, "rows", "cols"), P("rows", "cols")),
        check_vma=False,
    )
```

```python
import functools

import jax
import jax.numpy as jnp
from jax import lax
from jax.experimental import pallas as pl
from jax.experimental.pallas import tpu as pltpu
from jax.sharding import PartitionSpec as P

C = 64
SEG = 128
RG = 8
D1 = 2
D2 = 4
EPS = 1e-05
SHARP = 10.0
LOG2E = 1.4426950408889634
ROWS = 64
HALO = D1 + D2
SLOTS = 8
SLOT_ROWS = (ROWS + 2 * D2) // SLOTS
EDGE_TILES = SLOT_ROWS + 2 * D1
IMG_ROWS = ROWS + 2 * HALO
HID_ROWS = ROWS + 2 * D2
PLANE = 8
KEYS = 2 * PLANE + 1
MESH = pl.DeviceIdType.MESH
VROWS = 80


def lane_iota(shape):
    return lax.broadcasted_iota(jnp.int32, shape, len(shape) - 1)


def roll(x, shift):
    return pltpu.roll(x, shift % SEG, x.ndim - 1)


def features_kernel(
    ranges, images, w1_ref, w2_ref, found_out, disp_out,
    img, edge, from_left, from_right, xs, hid, hs, unit, w1, w2,
    queries, keys, acc, bias, found, disp, range_tiles, range_all,
    load_sem, row_send, row_recv, col_send, col_recv,
    spread_send, spread_recv, near_send, near_recv, far_send, far_recv, last_send, last_recv, own_sem,
    range_send, range_recv, found_send, found_recv, disp_send, disp_recv,
):
    row_count, col_count = lax.axis_size("rows"), lax.axis_size("cols")
    x, col = lax.axis_index("rows"), lax.axis_index("cols")
    me = lax.rem(col, PLANE)
    base = col - me
    lane = lane_iota((C, SEG))

    def at_row(step):
        return (lax.rem(x + step + row_count, row_count), col)

    def at_col(step):
        return (x, lax.rem(col + step + col_count, col_count))

    barrier = pltpu.get_barrier_semaphore()
    friends = [at_row(1), at_row(-1), at_col(1), at_col(-1), at_col(PLANE), at_col(-PLANE)]
    friends += [(x, base + lax.rem(me + o, PLANE)) for o in range(1, PLANE)]
    for friend in friends:
        pl.semaphore_signal(barrier, inc=1, device_id=friend, device_id_type=MESH)

    loads = [
        pltpu.make_async_copy(images.at[n], img.at[n, pl.ds(HALO, ROWS)], load_sem.at[n])
        for n in range(2)
    ]
    loads[1].start()
    loads[0].start()
    pl.semaphore_wait(barrier, len(friends))

    def remote(src, dst, send, recv, device):
        return pltpu.make_async_remote_copy(
            src_ref=src, dst_ref=dst, send_sem=send, recv_sem=recv,
            device_id=device, device_id_type=MESH,
        )

    def row_copies(n):
        return (
            remote(
                images.at[n, pl.ds(ROWS - HALO, HALO)], img.at[n, pl.ds(0, HALO)],
                row_send.at[n, 0], row_recv.at[n, 0], at_row(1),
            ),
            remote(
                images.at[n, pl.ds(0, HALO)], img.at[n, pl.ds(HALO + ROWS, HALO)],
                row_send.at[n, 1], row_recv.at[n, 1], at_row(-1),
            ),
        )

    def col_copies(n):
        return (
            remote(edge.at[n], from_left.at[n], col_send.at[n, 0], col_recv.at[n, 0], at_col(1)),
            remote(edge.at[n], from_right.at[n], col_send.at[n, 1], col_recv.at[n, 1], at_col(-1)),
        )

    for copy in row_copies(1):
        copy.start()

    for group in range(PLANE):
        tile_row = lax.broadcasted_iota(jnp.int32, (8, SEG), 0)
        range_tiles[group] = jnp.where(tile_row == 0, ranges[0, group], ranges[1, group])

    def send_range(peer, slot):
        return remote(
            range_tiles.at[peer], range_all.at[slot],
            range_send.at[peer], range_recv.at[slot], (x, base + peer),
        )

    def start_range(o, carry):
        send_range(lax.rem(me + o, PLANE), me).start()
        return carry

    lax.fori_loop(1, PLANE, start_range, 0)
    range_all[me] = range_tiles[me]

    for ref, out in ((w1_ref, w1), (w2_ref, w2)):
        taps = jnp.concatenate([ref[t] for t in range(9)], axis=1)
        none = jnp.zeros((C, 3 * C), jnp.bfloat16)
        out[0:C] = jnp.concatenate([taps, none], axis=1)
        out[C:] = jnp.concatenate([none, taps], axis=1)

    def send_edges(n):
        loads[n].wait()
        for copy in row_copies(n):
            copy.wait()

        @pl.when(x == 0)
        def _():
            img[n, 0:HALO] = jnp.zeros((HALO, C, SEG), jnp.bfloat16)

        @pl.when(x == row_count - 1)
        def _():
            img[n, HALO + ROWS :] = jnp.zeros((HALO, C, SEG), jnp.bfloat16)

        def pack(tile, carry):
            packed = jnp.zeros((C, SEG), jnp.bfloat16)
            for slot in range(SLOTS):
                row = img[n, SLOT_ROWS * slot + tile]
                start = 16 * slot
                packed = jnp.where((lane >= start) & (lane < start + 8), roll(row, start + 6), packed)
                packed = jnp.where((lane >= start + 8) & (lane < start + 16), roll(row, start + 10), packed)
            edge[n, tile] = packed
            return carry

        lax.fori_loop(0, EDGE_TILES, pack, 0)
        for copy in col_copies(n):
            copy.start()

    send_edges(1)
    for copy in row_copies(0):
        copy.start()

    climbs = 1 - lax.rem(me, 2)

    def group_at(s):
        return lax.rem(me + 2 * PLANE + (2 * climbs - 1) * s, PLANE)

    part = lane % 16
    inner = (part >= 6) & (part < 10)
    low_part = part < 6
    left_open = jnp.where(col == 0, 0.0, 1.0)
    right_open = jnp.where(col == col_count - 1, 0.0, 1.0)
    open_side = jnp.where(part < 8, left_open, right_open)
    first_row = x * ROWS - D2
    height = row_count * ROWS
    slot_row = SLOT_ROWS * (lane // 16) + first_row

    def shifted(read, edges, rows, dest, dilation, first_left, first_right):
        for slot in range(SLOTS):
            low = slot * SLOT_ROWS
            high = rows if slot == SLOTS - 1 else low + SLOT_ROWS

            def one(row, carry, slot=slot, low=low):
                value = read(row)
                tile = edges(row - low)
                dest[row, 0:C] = jnp.where(
                    lane < dilation, roll(tile, -(16 * slot + first_left)), roll(value, dilation)
                )
                dest[row, C : 2 * C] = value
                dest[row, 2 * C :] = jnp.where(
                    lane >= SEG - dilation,
                    roll(tile, SEG - dilation - 16 * slot - first_right),
                    roll(value, -dilation),
                )
                return carry

            lax.fori_loop(low, high, one, 0, unroll=3)

    def window(ref, row, step, count):
        return jnp.concatenate([ref[row + step * t] for t in range(count)], axis=0)

    def pairs(weights, ref, rows, step):
        both = jnp.concatenate([window(ref, row, step, 4) for row in rows], axis=1)
        return jnp.dot(weights[...], both, preferred_element_type=jnp.float32)

    def silu(v):
        half = 0.5 * v
        return half + half * jnp.tanh(half)

    def spread(n, group):
        out = keys.at[2 * PLANE + 1 + me] if n else queries.at[me]
        return remote(
            unit.at[n, pl.ds(RG * group, RG)], out,
            spread_send.at[n, group], spread_recv.at[n, me], (x, base + group),
        )

    def arrived(n, source):
        out = keys.at[2 * PLANE + 1 + source] if n else queries.at[source]
        remote(
            unit.at[n, pl.ds(RG * source, RG)], out,
            spread_send.at[n, source], spread_recv.at[n, source], (x, base + source),
        ).wait_recv()

    def convolve(n, middle, each, shifts_done, after):
        for copy in col_copies(n):
            copy.wait()

        def merge(tile, carry):
            ours = edge[n, tile]
            left = from_left[n, tile] * left_open.astype(jnp.bfloat16)
            right = from_right[n, tile] * right_open.astype(jnp.bfloat16)
            value = jnp.where(inner, ours, jnp.where(low_part, left, right))
            edge[n, tile] = value
            dest = IMG_ROWS + tile
            xs[dest, 0:C] = roll(value, D1)
            xs[dest, C : 2 * C] = value
            xs[dest, 2 * C :] = roll(value, -D1)
            return carry

        lax.fori_loop(0, EDGE_TILES, merge, 0)
        shifted(lambda row: img[n, row], lambda t: edge[n, t], IMG_ROWS, xs, D1, 4, 10)
        shifts_done()
        def packed_hidden(tile, act):
            at = slot_row + tile
            inside = jnp.where((at >= 0) & (at < height), open_side, 0.0)
            hid[HID_ROWS + tile] = (act * inside).astype(jnp.bfloat16)

        def conv1_packed(step, carry):
            tile = 4 * step
            act = silu(pairs(w1, xs, (IMG_ROWS + tile, IMG_ROWS + tile + 1), D1))
            for a in range(2):
                for b in range(2):
                    value = act[C * a : C * (a + 1), SEG * b : SEG * (b + 1)]
                    packed_hidden(tile + 2 * a + b, value)
            return carry

        lax.fori_loop(0, SLOT_ROWS // 4, conv1_packed, 0, unroll=2)
        tile = SLOT_ROWS - 1
        end = window(xs, IMG_ROWS + tile, D1, 3)
        packed_hidden(tile, silu(jnp.dot(w1[0:C, 0 : 9 * C], end, preferred_element_type=jnp.float32)))

        def hidden_rows(block):
            row = RG * block
            starts = (row, row + 1, row + 4, row + 5)
            act = silu(pairs(w1, xs, starts, D1))
            for a in range(2):
                for b, start in enumerate(starts):
                    at = first_row + start + 2 * a
                    inside = jnp.where((at >= 0) & (at < height), 1.0, 0.0)
                    value = act[C * a : C * (a + 1), SEG * b : SEG * (b + 1)] * inside
                    value = value.astype(jnp.bfloat16)
                    hid[start + 2 * a] = value
            for step in range(RG):
                at = row + step
                slot = at // SLOT_ROWS
                value = hid[at]
                tile = hid[HID_ROWS + at - SLOT_ROWS * slot]
                from_low = pltpu.roll(tile, lax.rem(2 * SEG - 16 * slot - 2, SEG), 1)
                from_high = pltpu.roll(tile, lax.rem(2 * SEG - D2 - 16 * slot - 10, SEG), 1)
                hs[at, 0:C] = jnp.where(lane < D2, from_low, roll(value, D2))
                hs[at, C : 2 * C] = value
                hs[at, 2 * C :] = jnp.where(lane >= SEG - D2, from_high, roll(value, -D2))

        def unit_rows(group):
            row = RG * group
            total = pairs(w2, hs, (row, row + 1, row + 2, row + 3), D2)
            for a in range(2):
                for b in range(4):
                    at = row + 4 * a + b
                    value = total[C * a : C * (a + 1), SEG * b : SEG * (b + 1)]
                    feats = (img[n, HALO + at].astype(jnp.float32) + value).astype(jnp.bfloat16)
                    feats = feats.astype(jnp.float32)
                    scale = lax.rsqrt(jnp.mean(feats * feats, axis=0, keepdims=True) + EPS)
                    unit[n, at] = (feats * scale).astype(jnp.bfloat16)

        def step(s, carry, act=None):
            group = group_at(s)
            unit_rows(group)
            following = group_at(s + 1)
            hidden_rows(following + climbs)

            @pl.when(following == (PLANE - 1) * (1 - climbs))
            def _():
                hidden_rows(PLANE * (1 - climbs))

            @pl.when(s > 0)
            def _():
                spread(n, group).start()

            if act is not None:
                act(s)
            return carry

        hidden_rows(me)
        hidden_rows(me + 1)
        step(0, 0)
        after(0)
        lax.fori_loop(1, 3, step, 0)
        middle()
        lax.fori_loop(3, PLANE - 1, functools.partial(step, act=each), 0)
        group = group_at(PLANE - 1)
        unit_rows(group)
        spread(n, group).start()
        after(1)

    def near(block, src):
        return remote(
            src, keys.at[PLANE + 1 + block], near_send.at[block], near_recv.at[block], at_col(PLANE)
        )

    def far(block):
        return remote(
            keys.at[PLANE + 1 + block], keys.at[1 + block],
            far_send.at[block], far_recv.at[block], at_col(PLANE),
        )

    last = remote(keys.at[PLANE], keys.at[0], last_send, last_recv, at_col(PLANE))
    own_k = pltpu.make_async_copy(
        unit.at[1, pl.ds(RG * me, RG)], keys.at[2 * PLANE + 1 + me], own_sem.at[1]
    )

    def block_of(o):
        return lax.rem(me + o, PLANE)

    def forward(age):
        block = lax.rem(me + PLANE + (2 * lax.rem(me + age, 2) - 1) * age, PLANE)
        arrived(1, block)
        near(block, keys.at[2 * PLANE + 1 + block]).start()

    def right_each(s):
        @pl.when(s >= PLANE - 3)
        def _():
            forward(s - (PLANE - 4))

    def right_after(stage):
        if stage == 0:
            own_k.start()
            near(me, unit.at[1, pl.ds(RG * me, RG)]).start()

    def left_shifts():
        forward(3)
        forward(4)

    def left_after(stage):
        if stage == 0:
            forward(5)
            forward(6)


    def relay(blocks):
        for block in blocks:
            near(block, keys.at[2 * PLANE + 1 + block]).wait_recv()
            far(block).start()

    convolve(1, lambda: send_edges(0), right_each, lambda: None, right_after)
    convolve(0, lambda: forward(7), None, left_shifts, left_after)
    relay((7, 6, 5, 4))
    own_q = pltpu.make_async_copy(unit.at[0, pl.ds(RG * me, RG)], queries.at[me], own_sem.at[0])
    own_q.start()

    def finish_spread(o, carry):
        block = block_of(o)
        arrived(0, block)
        send_range(block, block).wait_recv()
        send_range(block, block).wait_send()
        for n in range(2):
            spread(n, block).wait_send()
        return carry

    lax.fori_loop(1, PLANE, finish_spread, 0)
    own_k.wait()
    own_q.wait()

    scale = SHARP / C * LOG2E
    plane = col // PLANE
    top = 2 * PLANE + 1

    def attend(first_key, key_blocks, first_q, q_blocks, needed, fresh, unroll):
        width, depth = q_blocks * SEG, key_blocks * SEG
        span = pl.ds(first_q * SEG, width)
        within = lane_iota((1, SEG))
        upper = jnp.concatenate(
            [SEG * (top + q - range_all[q, 0:1]) + within for q in range(first_q, first_q + q_blocks)],
            axis=1,
        )
        lower = jnp.concatenate(
            [
                SEG * (top + q - range_all[q, 0:1] - range_all[q, 1:2]) + within
                for q in range(first_q, first_q + q_blocks)
            ],
            axis=1,
        )

        def mask(step, carry):
            at = 64 * step
            key = SEG * first_key + at + lax.broadcasted_iota(jnp.int32, (64, width), 0)
            inside = (key <= upper) & (key > lower)
            bias[pl.ds(pl.multiple_of(at, 64), 64), 0:width] = jnp.where(inside, 0.0, -1e30)
            return carry

        lax.fori_loop(0, depth // 64, mask, 0)
        present = jnp.where(plane >= needed, 1.0, 0.0).astype(jnp.bfloat16)
        extra_row = lax.broadcasted_iota(jnp.int32, (16, SEG), 0)
        column = lane_iota((16, SEG)).astype(jnp.float32)
        extra = jnp.concatenate(
            [
                jnp.where(
                    extra_row == 0,
                    1.0,
                    jnp.where(extra_row == 1, column, jnp.where(extra_row == 2, float(first_key + b), 0.0)),
                )
                for b in range(key_blocks)
            ],
            axis=1,
        ).astype(jnp.bfloat16)

        def one_row(row, carry):
            chunk = jnp.concatenate([keys[first_key + b, row] for b in range(key_blocks)], axis=1)
            if needed:
                chunk = chunk * present
            q = jnp.concatenate([queries[first_q + b, row] for b in range(q_blocks)], axis=1)
            s = jnp.dot(chunk.T, q, preferred_element_type=jnp.float32)
            p = jnp.exp2(s * scale + bias[0:depth, 0:width]).astype(jnp.bfloat16)
            values = jnp.concatenate([chunk, extra], axis=0)
            total = jnp.dot(values, p, preferred_element_type=jnp.float32)
            if fresh:
                acc[row, :, span] = total
            else:
                acc[row, :, span] += total
            return carry

        lax.fori_loop(0, RG, one_row, 0, unroll=unroll)

    def give_back(peer, slot):
        return [
            remote(
                found.at[peer], found_out.at[slot],
                found_send.at[peer], found_recv.at[slot], (x, base + peer),
            ),
            remote(
                disp.at[peer], disp_out.at[slot],
                disp_send.at[peer], disp_recv.at[slot], (x, base + peer),
            ),
        ]

    def keep(slot):
        return [
            pltpu.make_async_copy(found.at[slot], found_out.at[slot], own_sem.at[2]),
            pltpu.make_async_copy(disp.at[slot], disp_out.at[slot], own_sem.at[3]),
        ]

    def conclude(first_q, q_blocks):
        column = lane_iota((1, SEG)).astype(jnp.float32)
        for q in range(first_q, first_q + q_blocks):

            def one_row(row, carry, q=q):
                t = acc[row, :, q * SEG : (q + 1) * SEG]
                inverse = 1.0 / t[C : C + 1]
                found[q, row] = (t[:C] * inverse).astype(jnp.bfloat16)
                hops = float(top + q) - t[C + 2 : C + 3] * inverse
                within = column - t[C + 1 : C + 2] * inverse
                disp[q, pl.ds(row, 1)] = hops + within * (1.0 / SEG)
                return carry

            lax.fori_loop(0, RG, one_row, 0, unroll=4)

            @pl.when(q != me)
            def _(q=q):
                for copy in give_back(q, me):
                    copy.start()

            @pl.when(q == me)
            def _(q=q):
                for copy in keep(q):
                    copy.start()

    attend(top, 4, 0, PLANE, 0, True, 4)
    relay((3, 2))
    far(7).wait_recv()
    last.start()
    attend(top + 4, 4, 4, 4, 0, False, 8)
    relay((1, 0))
    attend(PLANE + 5, 4, 0, PLANE, 1, False, 4)
    attend(PLANE + 1, 4, 0, PLANE, 1, False, 4)
    far(6).wait_recv()
    far(5).wait_recv()
    attend(6, 3, 0, 8, 2, False, 4)
    conclude(6, 2)
    far(4).wait_recv()
    far(3).wait_recv()
    attend(4, 2, 0, 6, 2, False, 8)
    conclude(4, 2)
    far(2).wait_recv()
    far(1).wait_recv()
    far(0).wait_recv()
    attend(1, 3, 0, 4, 2, False, 8)
    conclude(1, 3)
    last.wait()
    attend(0, 1, 0, 1, 3, False, 8)
    conclude(0, 1)

    def sent(block, carry):
        near(block, keys.at[2 * PLANE + 1 + block]).wait_send()
        far(block).wait_send()
        return carry

    lax.fori_loop(0, PLANE, sent, 0)

    def returned(o, carry):
        for copy in give_back(block_of(o), block_of(o)):
            copy.wait_send()
            copy.wait_recv()
        return carry

    lax.fori_loop(1, PLANE, returned, 0)
    for copy in keep(me):
        copy.wait()


def features(ranges, images, w1, w2):
    anywhere = pl.BlockSpec(memory_space=pl.ANY)
    vmem = pl.BlockSpec(memory_space=pltpu.VMEM)
    dma = pltpu.SemaphoreType.DMA
    bf16 = jnp.bfloat16
    return pl.pallas_call(
        features_kernel,
        in_specs=[pl.BlockSpec(memory_space=pltpu.SMEM), anywhere, vmem, vmem],
        out_specs=(anywhere, anywhere),
        out_shape=(
            jax.ShapeDtypeStruct((PLANE, RG, C, SEG), bf16),
            jax.ShapeDtypeStruct((PLANE, RG, SEG), jnp.float32),
        ),
        scratch_shapes=[
            pltpu.VMEM((2, IMG_ROWS, C, SEG), bf16),
            pltpu.VMEM((2, EDGE_TILES, C, SEG), bf16),
            pltpu.VMEM((2, EDGE_TILES, C, SEG), bf16),
            pltpu.VMEM((2, EDGE_TILES, C, SEG), bf16),
            pltpu.VMEM((IMG_ROWS + EDGE_TILES, 3 * C, SEG), bf16),
            pltpu.VMEM((HID_ROWS + SLOT_ROWS, C, SEG), bf16),
            pltpu.VMEM((HID_ROWS, 3 * C, SEG), bf16),
            pltpu.VMEM((2, ROWS, C, SEG), bf16),
            pltpu.VMEM((2 * C, 12 * C), bf16),
            pltpu.VMEM((2 * C, 12 * C), bf16),
            pltpu.VMEM((PLANE, RG, C, SEG), bf16),
            pltpu.VMEM((KEYS + PLANE, RG, C, SEG), bf16),
            pltpu.VMEM((RG, VROWS, PLANE * SEG), jnp.float32),
            pltpu.VMEM((4 * SEG, PLANE * SEG), jnp.float32),
            pltpu.VMEM((PLANE, RG, C, SEG), bf16),
            pltpu.VMEM((PLANE, RG, SEG), jnp.float32),
            pltpu.VMEM((PLANE, 8, SEG), jnp.int32),
            pltpu.VMEM((PLANE, 8, SEG), jnp.int32),
            dma((2,)), dma((2, 2)), dma((2, 2)), dma((2, 2)), dma((2, 2)),
            dma((2, PLANE)), dma((2, PLANE)),
            dma((PLANE,)), dma((PLANE,)), dma((PLANE,)), dma((PLANE,)),
            dma, dma, dma((4,)),
            dma((PLANE,)), dma((PLANE,)), dma((PLANE,)), dma((PLANE,)), dma((PLANE,)), dma((PLANE,)),
        ],
        compiler_params=pltpu.CompilerParams(
            collective_id=0, has_side_effects=True, vmem_limit_bytes=48 * 1024 * 1024
        ),
        name="features",
    )(ranges, images, w1, w2)


def per_device(images, first_weight, second_weight, search_ranges):
    matched, disparity = features(
        search_ranges[:, :, 0], images.transpose(0, 2, 1, 3), first_weight, second_weight
    )
    return (
        matched.reshape(ROWS, C, SEG).transpose(1, 0, 2),
        disparity.reshape(ROWS, SEG),
    )


def solution(mesh):
    placed = (P(None, None, "rows", "cols"), P(), P(), P(None, "rows", "cols"))
    return jax.shard_map(
        per_device,
        mesh=mesh,
        in_specs=placed,
        out_specs=(P(None, "rows", "cols"), P("rows", "cols")),
        check_vma=False,
    )
```
